32 devices in a mesh: dp: 8 (over z, x), head: 4 (over y, core).
Axes of the slice: x: 2, y: 2, z: 4, core: 2. Of those that a mesh axis runs over, the one named last changes fastest.
Arguments:
- tokens: float32 [4096, 1024], P(('dp', 'head')), may hold values from -16 to 16
- cotangent: float32 [4096, 1024], P('dp'), may hold values from -16 to 16
- lengths: int32 [4], replicated, may hold values from 0 to 2048, as said below
- w_qkvu: float32 [2, 4, 1024, 1024], P(None, None, 'dp', 'head'), may hold values from -0.1875 to 0.1875
- w_out: float32 [2, 1024, 1024], P(None, 'head', 'dp'), may hold values from -0.1875 to 0.1875
- w_gu: float32 [2, 2, 1024, 2816], P(None, None, 'dp', 'head'), may hold values from -0.1875 to 0.1875
- w_down: float32 [2, 2816, 1024], P(None, 'head', 'dp'), may hold values from -0.109375 to 0.109375
- m_qkvu: float32 [2, 4, 1024, 1024], P(None, None, 'dp', 'head'), may hold values from -0.013671875 to 0.013671875
- m_out: float32 [2, 1024, 1024], P(None, 'head', 'dp'), may hold values from -0.013671875 to 0.013671875
- m_gu: float32 [2, 2, 1024, 2816], P(None, None, 'dp', 'head'), may hold values from -0.013671875 to 0.013671875
- m_down: float32 [2, 2816, 1024], P(None, 'head', 'dp'), may hold values from -0.013671875 to 0.013671875
- e_qkvu: float32 [2, 4, 1024, 1024], P(None, None, 'dp', 'head'), may hold values from -0.1875 to 0.1875
- e_out: float32 [2, 1024, 1024], P(None, 'head', 'dp'), may hold values from -0.1875 to 0.1875
- e_gu: float32 [2, 2, 1024, 2816], P(None, None, 'dp', 'head'), may hold values from -0.1875 to 0.1875
- e_down: float32 [2, 2816, 1024], P(None, 'head', 'dp'), may hold values from -0.109375 to 0.109375
Outputs:
- out_tokens: float32 [4096, 1024], P(('dp', 'head'))
- grad_tokens: float32 [4096, 1024], P(('dp', 'head'))
- grad_norm: float32 [], replicated
- new_m_qkvu: float32 [2, 4, 1024, 1024], P(None, None, 'dp', 'head')
- new_m_out: float32 [2, 1024, 1024], P(None, 'head', 'dp')
- new_m_gu: float32 [2, 2, 1024, 2816], P(None, None, 'dp', 'head')
- new_m_down: float32 [2, 2816, 1024], P(None, 'head', 'dp')
- new_e_qkvu: float32 [2, 4, 1024, 1024], P(None, None, 'dp', 'head')
- new_e_out: float32 [2, 1024, 1024], P(None, 'head', 'dp')
- new_e_gu: float32 [2, 2, 1024, 2816], P(None, None, 'dp', 'head')
- new_e_down: float32 [2, 2816, 1024], P(None, 'head', 'dp')
- new_w_qkvu: float32 [2, 4, 1024, 1024], P(None, None, 'dp', 'head')
- new_w_out: float32 [2, 1024, 1024], P(None, 'head', 'dp')
- new_w_gu: float32 [2, 2, 1024, 2816], P(None, None, 'dp', 'head')
- new_w_down: float32 [2, 2816, 1024], P(None, 'head', 'dp')
The draws below stay inside these ranges and needn't reach their ends.
Inputs may be any that keep to these rules, and one draw needn't show every extreme that they name: `lengths`: sequences lie end to end from row 0 in the order listed; every nonzero entry is 1024 or more, zeros stand only after the last nonzero entry and at least the last entry is zero, the entries sum to at most 4096, and in every draw one sequence has exactly 2048 tokens.
All inputs are finite; a program needn't handle non-finite values.
Results may differ from the reference program's by a relative error of at most 0.03.
Values may be sent and summed in bfloat16 or wider, within the bound.
No kernel may reach another device: no remote copies, remote signals or barrier semaphores. Data moves between devices by JAX's collectives and lax.ppermute only.
A program may use at most 192 MiB of HBM per device.

```python
import math
from functools import partial
import jax
import jax.numpy as jnp
from jax import lax

D = 1024
HEADS = 8
HEAD_DIM = 128
FF = 2816
DEPTH = 24
LAYERS = 2
FIRST_LAYER = 21
SHORTEST = 1024
CAP = 512
TOKENS = 4096
LONGEST = 2048
SEQS = 4
N_DP = 8


def draw_lengths(key, part):
    first_key = jax.random.fold_in(key, 21)
    second_key = jax.random.fold_in(key, 22)
    extra_key = jax.random.fold_in(key, 23)
    spot_key = jax.random.fold_in(key, 24)
    first_level = jax.random.randint(first_key, (SEQS,), 0, 4)
    second_level = jax.random.randint(second_key, (SEQS,), 0, 4)
    level_pick = jnp.minimum(first_level, second_level)
    multiple = jnp.array([1, 2, 4, 8], dtype=jnp.int32)[level_pick]
    extra = jax.random.randint(extra_key, (SEQS,), 0, SHORTEST)
    raw_lengths = jnp.minimum(SHORTEST * multiple + extra, LONGEST)
    spot = jax.random.randint(spot_key, (), 0, 2)
    positions = jnp.arange(SEQS, dtype=jnp.int32)
    raw_lengths = jnp.where(positions == spot, LONGEST, raw_lengths)
    running = jnp.cumsum(raw_lengths)
    return jnp.where(running <= TOKENS, raw_lengths, 0).astype(jnp.int32)


def column_field(key, salt):
    value_key = jax.random.fold_in(key, salt)
    ramp = jnp.arange(D, dtype=jnp.float32) / (D - 1.0)
    scales = jnp.exp(jnp.log(6.0) * ramp)
    scales = scales * jax.lax.rsqrt(jnp.mean(scales * scales))
    values = jnp.clip(jax.random.normal(value_key, (TOKENS, D), jnp.float32), -6.0, 6.0)
    return jnp.clip(values * scales[None, :], -16.0, 16.0)


def draw_tokens(key, part):
    return column_field(key, 31)


def draw_cotangent(key, part):
    return column_field(key, 41)


def block_scale(own_key, dims, shards, smallest, largest):
    gain = 1.0
    for axis_at, parts in shards:
        steps = jax.random.uniform(jax.random.fold_in(jax.random.fold_in(own_key, 6), axis_at), (parts,), jnp.float32, smallest / len(shards), largest / len(shards))
        gain = gain * jnp.repeat(jnp.exp(steps), dims[axis_at] // parts).reshape((-1,) + (1,) * (len(dims) - 1 - axis_at))
    return gain


def normal_values(stream_key, dims, scale, bound, pieces=(), kind=jnp.bfloat16):
    values = scale * jax.random.normal(stream_key, dims, jnp.float32)
    if pieces:
        values = values * block_scale(stream_key, dims, pieces, -0.22, 0.18)
    return jnp.clip(values, -bound, bound).astype(kind)


def setup_inputs(seed: int = 0) -> dict:
    key_list = jax.random.split(jax.random.key(seed), 16)
    return {
        "tokens": draw_tokens(jax.random.fold_in(key_list[15], 71), 0),
        "cotangent": draw_cotangent(jax.random.fold_in(key_list[15], 71), 0),
        "lengths": draw_lengths(jax.random.fold_in(key_list[15], 71), 0),
        "w_qkvu": normal_values(key_list[3], (LAYERS, 4, D, D), D ** -0.5, 0.1875, ((2, 8), (3, 4)), jnp.float32),
        "w_out": normal_values(key_list[4], (LAYERS, D, D), D ** -0.5, 0.1875, ((1, 4), (2, 8)), jnp.float32),
        "w_gu": normal_values(key_list[5], (LAYERS, 2, D, FF), D ** -0.5, 0.1875, ((2, 8), (3, 4)), jnp.float32),
        "w_down": normal_values(key_list[6], (LAYERS, FF, D), FF ** -0.5, 0.109375, ((1, 4), (2, 8)), jnp.float32),
        "m_qkvu": normal_values(key_list[7], (LAYERS, 4, D, D), (5 * (LAYERS * (5 * D * D + 3 * D * FF)) ** -0.5), 0.013671875, ((2, 8), (3, 4)), jnp.float32),
        "m_out": normal_values(key_list[8], (LAYERS, D, D), (5 * (LAYERS * (5 * D * D + 3 * D * FF)) ** -0.5), 0.013671875, ((1, 4), (2, 8)), jnp.float32),
        "m_gu": normal_values(key_list[9], (LAYERS, 2, D, FF), (5 * (LAYERS * (5 * D * D + 3 * D * FF)) ** -0.5), 0.013671875, ((2, 8), (3, 4)), jnp.float32),
        "m_down": normal_values(key_list[10], (LAYERS, FF, D), (5 * (LAYERS * (5 * D * D + 3 * D * FF)) ** -0.5), 0.013671875, ((1, 4), (2, 8)), jnp.float32),
        "e_qkvu": normal_values(key_list[11], (LAYERS, 4, D, D), D ** -0.5, 0.1875, ((2, 8), (3, 4)), jnp.float32),
        "e_out": normal_values(key_list[12], (LAYERS, D, D), D ** -0.5, 0.1875, ((1, 4), (2, 8)), jnp.float32),
        "e_gu": normal_values(key_list[13], (LAYERS, 2, D, FF), D ** -0.5, 0.1875, ((2, 8), (3, 4)), jnp.float32),
        "e_down": normal_values(key_list[14], (LAYERS, FF, D), FF ** -0.5, 0.109375, ((1, 4), (2, 8)), jnp.float32),
    }


@jax.custom_vjp
def low(v):
    return lax.optimization_barrier(v.astype(jnp.bfloat16)).astype(jnp.float32)

@jax.custom_vjp
def low_back(v):
    return v

def low_keep(v):
    return (low(v), None)

def low_pass(kept, grad):
    return (grad,)

def back_keep(v):
    return (v, None)

def back_low(kept, grad):
    return (low(grad),)
low.defvjp(low_keep, low_pass)
low_back.defvjp(back_keep, back_low)
epsilon = 1e-06
highest = lax.Precision.HIGHEST

def simple_norm(values):
    return values * lax.rsqrt(lax.optimization_barrier(jnp.mean(values * values, axis=-1, keepdims=True)) + epsilon)

def packing(lengths, group_index, capacity):
    seq_ends = jnp.cumsum(lengths, dtype=jnp.int32)
    seq_starts = seq_ends - lengths
    first_place = group_index * capacity
    places = first_place + jnp.arange(capacity, dtype=jnp.int32)
    segment = lax.optimization_barrier(jnp.sum((places[:, None] >= seq_ends[None, :]).astype(jnp.int32), axis=1, dtype=jnp.int32))
    member = segment[:, None] == jnp.arange(lengths.shape[0], dtype=jnp.int32)[None, :]
    begins = lax.optimization_barrier(jnp.sum(jnp.where(member, seq_starts[None, :], 0), axis=1, dtype=jnp.int32))
    offset = (places - begins).astype(jnp.float32)
    live = segment < lengths.shape[0]
    previous = jnp.sum((first_place - 1 >= seq_ends).astype(jnp.int32), dtype=jnp.int32)
    return (segment, offset, live, previous)

def carry_masks(segment, live, previous, slopes):
    row_count = segment.shape[0]
    positions = jnp.arange(row_count, dtype=jnp.float32)
    inward = (segment == previous) & live
    outward = (segment == segment[row_count - 1]) & live
    joined = (segment[0] == segment[row_count - 1]) & live[row_count - 1]
    query_decay = jnp.where(inward[:, None], jnp.exp(-slopes[None, :] * (positions[:, None] + 1.0)), 0.0)
    key_decay = jnp.where(outward[:, None], jnp.exp(-slopes[None, :] * (row_count - 1.0 - positions[:, None])), 0.0)
    through = jnp.where(joined, jnp.exp(-slopes * row_count), 0.0)
    return (query_decay, key_decay, through)

def decay_table(segment, live, slopes):
    places = jnp.arange(segment.shape[0], dtype=jnp.float32)
    apart = places[:, None] - places[None, :]
    allowed = (apart >= 0.0) & (segment[:, None] == segment[None, :]) & live[:, None] & live[None, :]
    return jnp.where(allowed[None], jnp.exp(-slopes[:, None, None] * jnp.maximum(apart, 0.0)[None]), 0.0)

def rotate_pair(values, cosine, sine):
    return jnp.concatenate([values * cosine[:, None, :], values * sine[:, None, :]], axis=-1)

def group_mix(operands, slopes):
    query, keys, values, segment, live = operands
    decay = decay_table(segment, live, slopes)
    scores = low_back(jnp.einsum('shc,thc->hst', query, keys, precision=highest))
    weights = low(scores * decay)
    return jnp.einsum('hst,thc->shc', weights, values, precision=highest)

def carry_step(state, item):
    decay_factor, fresh_state = item
    return (decay_factor[:, None, None] * state + fresh_state, state)

def layer_slopes():
    base_slopes = jnp.exp2(-8.0 * jnp.arange(1, HEADS + 1, dtype=jnp.int32).astype(jnp.float32) / HEADS)
    depth_index = (FIRST_LAYER + jnp.arange(LAYERS, dtype=jnp.int32)).astype(jnp.float32)
    layer_scale = 1.0 - depth_index / (DEPTH - 1.0) + 1e-05
    return layer_scale[:, None] * base_slopes[None, :]

def forward(tokens, w_qkvu, w_out, w_gu, w_down, cosine, sine, segment, live, slopes, query_decay, key_decay, through):
    residual = tokens
    for level in range(LAYERS):
        mixer = jax.checkpoint(partial(group_mix, slopes=slopes[level]))
        hidden = low(simple_norm(residual))
        projected = low_back(jnp.einsum('td,kde->kte', hidden, low(w_qkvu[level]), precision=highest))
        query = low(rotate_pair(jax.nn.silu(projected[0]).reshape(TOKENS, HEADS, HEAD_DIM), cosine, sine))
        keys = low(rotate_pair(jax.nn.silu(projected[1]).reshape(TOKENS, HEADS, HEAD_DIM), cosine, sine))
        values = low(projected[2].reshape(TOKENS, HEADS, HEAD_DIM))
        query_groups = query.reshape(N_DP, CAP, HEADS, 2 * HEAD_DIM)
        key_groups = keys.reshape(N_DP, CAP, HEADS, 2 * HEAD_DIM)
        value_groups = values.reshape(N_DP, CAP, HEADS, HEAD_DIM)
        within = lax.map(mixer, (query_groups, key_groups, value_groups, segment, live))
        decayed = key_groups * key_decay[level][..., None]
        state_local = jnp.einsum('gthe,gthc->ghec', decayed, value_groups, precision=highest)
        empty_state = jnp.zeros((HEADS, 2 * HEAD_DIM, HEAD_DIM), dtype=jnp.float32)
        _, incoming = lax.scan(carry_step, empty_state, (through[level], state_local))
        carried = query_decay[level][..., None] * jnp.einsum('gshe,ghec->gshc', query_groups, incoming, precision=highest)
        mixed = low_back((within + carried).reshape(TOKENS, D))
        gated = low(simple_norm(mixed) * projected[3])
        residual = residual + low_back(jnp.dot(gated, low(w_out[level]), precision=highest, preferred_element_type=jnp.float32))
        hidden_ffn = low(simple_norm(residual))
        gate_up = low_back(jnp.einsum('td,kdf->ktf', hidden_ffn, low(w_gu[level]), precision=highest))
        product = low(gate_up[0] * gate_up[1])
        residual = residual + low_back(jnp.dot(product, low(w_down[level]), precision=highest, preferred_element_type=jnp.float32))
    return residual

def reference(tokens, cotangent, lengths, w_qkvu, w_out, w_gu, w_down, m_qkvu, m_out, m_gu, m_down, e_qkvu, e_out, e_gu, e_down):
    group_ids = jnp.arange(N_DP, dtype=jnp.int32)
    segment, offset, live, previous = jax.vmap(partial(packing, lengths, capacity=CAP))(group_ids)
    slopes = layer_slopes()
    masks = [jax.vmap(partial(carry_masks, slopes=slopes[level]))(segment, live, previous) for level in range(LAYERS)]
    query_decay = jnp.stack([masks[level][0] for level in range(LAYERS)])
    key_decay = jnp.stack([masks[level][1] for level in range(LAYERS)])
    through = jnp.stack([masks[level][2] for level in range(LAYERS)])
    frequency = jnp.exp(-math.log(10000.0) * jnp.arange(HEAD_DIM, dtype=jnp.float32) / HEAD_DIM)
    angles = offset.reshape(TOKENS)[:, None] * frequency[None, :]
    cosine = jnp.cos(angles)
    sine = jnp.sin(angles)
    runner = partial(forward, cosine=cosine, sine=sine, segment=segment, live=live, slopes=slopes, query_decay=query_decay, key_decay=key_decay, through=through)
    outputs, pullback = jax.vjp(runner, tokens, w_qkvu, w_out, w_gu, w_down)
    masked = cotangent * live.reshape(TOKENS)[:, None].astype(jnp.float32)
    grad_tokens, g_qkvu, g_out, g_gu, g_down = pullback(masked)
    squares = jnp.sum(g_qkvu * g_qkvu) + jnp.sum(g_out * g_out) + jnp.sum(g_gu * g_gu) + jnp.sum(g_down * g_down)
    grad_norm = jnp.sqrt(squares)
    factor = jnp.minimum(1.0, 1.0 / (grad_norm + 1e-06))
    rate = 0.1 * math.sqrt(LAYERS * (5 * D * D + 3 * D * FF) / D)

    def update(weight, moment, average, gradient):
        clipped = gradient * factor
        new_moment = 0.9 * moment + clipped
        new_weight = weight - rate * (clipped + 0.9 * new_moment)
        new_average = 0.8 * average + 0.2 * new_weight
        return (new_moment, new_average, new_weight)
    qa, qb, qc = update(w_qkvu, m_qkvu, e_qkvu, g_qkvu)
    oa, ob, oc = update(w_out, m_out, e_out, g_out)
    ga, gb, gc = update(w_gu, m_gu, e_gu, g_gu)
    da, db, dc = update(w_down, m_down, e_down, g_down)
    return (outputs, grad_tokens, grad_norm, qa, oa, ga, da, qb, ob, gb, db, qc, oc, gc, dc)
```

```python
import math

import jax
import jax.numpy as jnp
from jax import lax
from jax.sharding import PartitionSpec as P

D = 1024
HEADS = 8
HEAD_DIM = 128
FF = 2816
DEPTH = 24
LAYERS = 2
FIRST_LAYER = 21

epsilon = 1e-06
bf16 = jnp.bfloat16
f32 = jnp.float32


def dot_nn(a, b):
    return lax.dot_general(a, b, (((1,), (0,)), ((), ())), preferred_element_type=f32)


def dot_nt(a, b):
    return lax.dot_general(a, b, (((1,), (1,)), ((), ())), preferred_element_type=f32)


def dot_tn(a, b):
    return lax.dot_general(a, b, (((0,), (0,)), ((), ())), preferred_element_type=f32)


def ring_order(count):
    return list(range(0, count, 2)) + list(range(1, count, 2))[::-1]


def ring_pairs(count):
    order = ring_order(count)
    ahead = [(order[i], order[(i + 1) % count]) for i in range(count)]
    return ahead, [(b, a) for a, b in ahead]


def tie(value, *others):
    return lax.optimization_barrier((value,) + others)[0]


class Gather:
    def __init__(self, shard, count):
        self.pairs = ring_pairs(count)
        self.count = count
        self.hops = 0
        self.pieces = [shard] + [None] * (count - 1)
        self.moving = (shard, shard)

    def step(self):
        self.hops += 1
        k, count = self.hops, self.count
        ahead, behind = self.moving
        if k == count // 2:
            half = ahead.shape[0] // 2
            ahead, behind = ahead[:half], behind[half:]
        ahead = lax.ppermute(ahead, "dp", self.pairs[0])
        behind = lax.ppermute(behind, "dp", self.pairs[1])
        self.moving = (ahead, behind)
        if k == count // 2:
            self.pieces[k] = jnp.concatenate([ahead, behind], axis=0)
        else:
            self.pieces[k], self.pieces[count - k] = ahead, behind

    def after(self, *values):
        self.moving = lax.optimization_barrier(self.moving + values)[:2]

    def before(self, value):
        return tie(value, *self.moving)

    def whole(self):
        while self.hops < self.count // 2:
            self.step()
        return jnp.concatenate(self.pieces, axis=1)


class Scatter:
    def __init__(self, pieces, count):
        self.pairs = ring_pairs(count)
        self.count = count
        self.hops = 0
        self.pieces = pieces
        far = pieces[count // 2]
        half = far.shape[0] // 2
        self.moving = (far[half:], far[:half])

    def step(self):
        self.hops += 1
        k, count = self.count // 2 - self.hops, self.count
        ahead = lax.ppermute(self.moving[0], "dp", self.pairs[0]).astype(f32)
        behind = lax.ppermute(self.moving[1], "dp", self.pairs[1]).astype(f32)
        if self.hops == 1:
            ahead = jnp.concatenate([jnp.zeros(behind.shape, f32), ahead], axis=0)
            behind = jnp.concatenate([behind, jnp.zeros(behind.shape, f32)], axis=0)
        if k:
            ahead = (ahead + self.pieces[count - k].astype(f32)).astype(bf16)
            behind = (behind + self.pieces[k].astype(f32)).astype(bf16)
        self.moving = (ahead, behind)

    def after(self, *values):
        self.moving = lax.optimization_barrier(self.moving + values)[:2]

    def before(self, value):
        return tie(value, *self.moving)

    def total(self):
        while self.hops < self.count // 2:
            self.step()
        return self.pieces[0].astype(f32) + self.moving[0] + self.moving[1]


NEAR = [(0, 1), (1, 0), (2, 3), (3, 2)]
FAR = [(0, 2), (2, 0), (1, 3), (3, 1)]
CROSS = [(0, 3), (3, 0), (1, 2), (2, 1)]


def head_gather(block):
    far = lax.ppermute(block, "head", FAR)
    near = lax.ppermute(block, "head", NEAR)
    cross = lax.ppermute(far, "head", NEAR)
    return jnp.concatenate([block, near, far, cross], axis=0)


def head_gather_small(block):
    far = lax.ppermute(block, "head", FAR)
    near = lax.ppermute(block, "head", NEAR)
    cross = lax.ppermute(block, "head", CROSS)
    return [block, near, far, cross]


def head_sum(values, rows):
    own, near, far, cross = head_gather_small(values)

    def blocks(array, mask):
        return jnp.concatenate([array[(j ^ mask) * rows : (j ^ mask) * rows + rows] for j in range(4)])

    return own + blocks(near, 1) + blocks(far, 2) + blocks(cross, 3)


def head_scatter(partial):
    near = lax.ppermute(partial[1], "head", NEAR)
    cross = lax.ppermute(partial[3], "head", NEAR)
    to_far = (partial[2].astype(f32) + cross.astype(f32)).astype(bf16)
    far = lax.ppermute(to_far, "head", FAR)
    return partial[0].astype(f32) + near.astype(f32) + far.astype(f32)


def row_scale_of(values):
    return lax.rsqrt(jnp.mean(values * values, axis=-1, keepdims=True) + epsilon)


def norm_back(values, grads):
    factor = row_scale_of(values)
    inner = jnp.mean(values * grads, axis=-1, keepdims=True)
    return factor * grads - values * (factor * factor * factor) * inner


def silu(v):
    return v * jax.nn.sigmoid(v)


def segment_of(places, seq_ends):
    return jnp.sum((places[..., None] >= seq_ends).astype(jnp.int32), axis=-1, dtype=jnp.int32)


def carry_factor(free, first, after, decay):
    steps = jnp.maximum(after - first, 0)
    whole = free[jnp.maximum(after, first)] == free[first]
    return jnp.where(whole, jnp.exp(-decay * steps.astype(f32)), 0.0)


def scaled(factor, states):
    return factor[:, None, None] * states.astype(f32)


def carried(states, group, count, free, decay, forward):
    pair, side = group // 2, group % 2
    first = 2 * pair
    states = states.astype(bf16)
    other = lax.ppermute(states, "dp", [(i, i ^ 1) for i in range(count)])
    low = jnp.where(side == 0, states, other).astype(f32)
    high = jnp.where(side == 0, other, states).astype(f32)
    through_low = carry_factor(free, first, first + 1, decay)
    through_high = carry_factor(free, first + 1, first + 2, decay)
    if forward:
        both = scaled(through_high, low) + high
    else:
        both = low + scaled(through_low, high)
    both = both.astype(bf16)
    total = jnp.zeros(states.shape, f32)
    for s in range(1, count // 2):
        moved = lax.ppermute(both, "dp", [(i, i ^ (2 * s)) for i in range(count)])
        theirs = pair ^ s
        if forward:
            used = theirs < pair
            factor = carry_factor(free, 2 * theirs + 2, first, decay)
        else:
            used = theirs > pair
            factor = carry_factor(free, first + 2, 2 * theirs, decay)
        total = total + scaled(jnp.where(used, factor, 0.0), moved)
    if forward:
        inner = scaled(through_low, total) + low
        total = jnp.where(side == 0, total, inner)
    else:
        inner = scaled(through_high, total) + high
        total = jnp.where(side == 0, inner, total)
    return total.astype(bf16)


def unrotate(grad, raw, cosine, sine):
    active = grad[:, :HEAD_DIM] * cosine + grad[:, HEAD_DIM:] * sine
    sigma = jax.nn.sigmoid(raw)
    return active * (sigma * (1.0 + raw * (1.0 - sigma)))


def per_device(
    tokens,
    cotangent,
    lengths,
    w_qkvu,
    w_out,
    w_gu,
    w_down,
    m_qkvu,
    m_out,
    m_gu,
    m_down,
    e_qkvu,
    e_out,
    e_gu,
    e_down,
):
    rows = tokens.shape[0]
    count = lax.axis_size("dp")
    ranks = lax.axis_size("head")
    group = lax.axis_index("dp")
    rank = lax.axis_index("head")
    capacity = rows * ranks
    local_heads = HEADS // ranks
    att = local_heads * HEAD_DIM
    ffw = FF // ranks
    part = D // count

    order = ring_order(count)
    place = [order.index(i) for i in range(count)]
    my_place = jnp.array(place, jnp.int32)[group]
    owners = [jnp.array(order, jnp.int32)[(my_place - k) % count] for k in range(count)]
    sources = [(my_place - place[c]) % count for c in range(count)]

    def to_ring(array):
        return jnp.concatenate(
            [lax.dynamic_slice_in_dim(array, owners[k] * part, part, 1) for k in range(count)], axis=1
        )

    def from_ring(array):
        return jnp.concatenate(
            [lax.dynamic_slice_in_dim(array, sources[c] * part, part, 1) for c in range(count)], axis=1
        )

    def flat(array):
        return jnp.swapaxes(array, -1, -2).reshape(-1, part).astype(bf16)

    gathers = []
    for level in range(LAYERS):
        key_value = flat(w_qkvu[level, 1:3])
        query_out = jnp.concatenate(
            [flat(w_qkvu[level, 0]), flat(w_qkvu[level, 3]), w_out[level].astype(bf16)]
        )
        gated_unit = jnp.concatenate([flat(w_gu[level]), w_down[level].astype(bf16)])
        gathers.append([Gather(x, count) for x in (key_value, query_out, gated_unit)])
    hops = count // 2
    for _ in range(hops):
        gathers[0][0].step()
        gathers[0][1].step()

    seq_ends = jnp.cumsum(lengths, dtype=jnp.int32)
    seq_starts = seq_ends - lengths
    seqs = lengths.shape[0]
    local = jnp.concatenate(
        [(rank ^ j) * rows + jnp.arange(rows, dtype=jnp.int32) for j in range(ranks)]
    )
    first_place = group * capacity
    places = first_place + local
    segment = segment_of(places, seq_ends)
    live = segment < seqs
    member = segment[:, None] == jnp.arange(seqs, dtype=jnp.int32)[None, :]
    begins = jnp.sum(jnp.where(member, seq_starts[None, :], 0), axis=1, dtype=jnp.int32)
    offset = (places - begins).astype(f32)
    previous = segment_of(first_place - 1, seq_ends)
    last = segment_of(first_place + capacity - 1, seq_ends)
    firsts = segment_of(jnp.arange(count, dtype=jnp.int32) * capacity, seq_ends)
    lasts = segment_of(jnp.arange(1, count + 1, dtype=jnp.int32) * capacity - 1, seq_ends)
    apart_groups = ((firsts != lasts) | (lasts >= seqs)).astype(jnp.int32)
    free = jnp.concatenate([jnp.zeros((1,), jnp.int32), jnp.cumsum(apart_groups, dtype=jnp.int32)])
    head_ids = rank * local_heads + jnp.arange(local_heads, dtype=jnp.int32)
    base_slopes = jnp.exp2(-8.0 * (head_ids + 1).astype(f32) / HEADS)
    depth_index = (FIRST_LAYER + jnp.arange(LAYERS, dtype=jnp.int32)).astype(f32)
    layer_scale = 1.0 - depth_index / (DEPTH - 1.0) + 1e-05
    frequency = jnp.exp(-math.log(10000.0) * jnp.arange(HEAD_DIM, dtype=f32) / HEAD_DIM)
    angles = offset[:, None] * frequency[None, :]
    cosine, sine = jnp.cos(angles), jnp.sin(angles)
    position = local.astype(f32)
    apart = position[:, None] - position[None, :]
    allowed = (
        (apart >= 0.0) & (segment[:, None] == segment[None, :]) & live[:, None] & live[None, :]
    )
    inward = (segment == previous) & live
    outward = (segment == last) & live

    residual = to_ring(tokens)
    stored = []
    for level in range(LAYERS):
        g_kv, g_quo, g_ffn = gathers[level]
        slopes = layer_scale[level] * base_slopes
        decay = jnp.where(
            allowed[None], jnp.exp(-slopes[:, None, None] * jnp.maximum(apart, 0.0)[None]), 0.0
        )
        query_decay = jnp.where(
            inward[:, None], jnp.exp(-slopes[None, :] * (position[:, None] + 1.0)), 0.0
        )
        key_decay = jnp.where(
            outward[:, None], jnp.exp(-slopes[None, :] * (capacity - 1.0 - position[:, None])), 0.0
        )
        x_att = residual
        hidden = head_gather((x_att * row_scale_of(x_att)).astype(bf16))
        w_kv = g_kv.whole()
        w_quo = g_quo.whole()
        if level == 0:
            g_ffn.after(w_kv, w_quo)
            g_ffn.step()
        projected = dot_nt(hidden, w_kv)
        k_raw, v_raw = projected[:, :att], projected[:, att:]
        heads = []
        for h in range(local_heads):
            cols = slice(h * HEAD_DIM, (h + 1) * HEAD_DIM)
            k_act = silu(k_raw[:, cols])
            keys = jnp.concatenate([k_act * cosine, k_act * sine], axis=1).astype(bf16)
            values = v_raw[:, cols].astype(bf16)
            decayed = (keys.astype(f32) * key_decay[:, h : h + 1]).astype(bf16)
            heads.append((keys, values, decayed, dot_tn(decayed, values)))
        states = jnp.stack([head[3] for head in heads])
        incoming = carried(states, group, count, free, slopes * capacity, True)
        projected = dot_nt(hidden, w_quo[: 2 * att])
        q_raw, u_raw = projected[:, :att], projected[:, att:]
        mixed, queries, weights = [], [], []
        for h in range(local_heads):
            cols = slice(h * HEAD_DIM, (h + 1) * HEAD_DIM)
            q_act = silu(q_raw[:, cols])
            query = jnp.concatenate([q_act * cosine, q_act * sine], axis=1).astype(bf16)
            keys, values, decayed, _ = heads[h]
            weight = (dot_nt(query, keys) * decay[h]).astype(bf16)
            within = dot_nn(weight, values)
            mixed.append(within + query_decay[:, h : h + 1] * dot_nn(query, incoming[h]))
            queries.append(query)
            weights.append(weight)
        mixed = jnp.concatenate(mixed, axis=1)
        squares = jnp.sum(mixed * mixed, axis=1)
        row_scale = lax.rsqrt(head_sum(squares, rows) / D + epsilon)
        ungated = (mixed * u_raw).astype(bf16)
        g_ffn.step()
        partial = g_ffn.before(dot_nn(ungated, w_quo[2 * att :]).astype(bf16))
        branch = head_scatter(partial.reshape(ranks, rows, D))
        x_ffn = x_att + branch * row_scale[:rows, None]
        g_ffn.step()
        hidden_ffn = g_ffn.before((x_ffn * row_scale_of(x_ffn)).astype(bf16))
        hidden_ffn = head_gather(hidden_ffn)
        w_ffn = g_ffn.whole()
        if level + 1 < LAYERS:
            next_kv, next_quo, next_ffn = gathers[level + 1]
            next_kv.after(w_ffn)
            next_kv.step()
            next_quo.after(w_ffn)
            next_quo.step()
        gate_up = dot_nt(hidden_ffn, w_ffn[: 2 * ffw])
        gate, up = gate_up[:, :ffw], gate_up[:, ffw:]
        product = (gate * up).astype(bf16)
        partial = dot_nn(product, w_ffn[2 * ffw :]).astype(bf16)
        if level + 1 < LAYERS:
            partial = next_quo.before(next_kv.before(partial))
            for _ in range(hops - 1):
                next_kv.step()
                next_quo.step()
            next_ffn.after(*next_kv.moving, *next_quo.moving)
            next_ffn.step()
        residual = x_ffn + head_scatter(partial.reshape(ranks, rows, D))
        stored.append(
            (
                x_att,
                x_ffn,
                hidden,
                (q_raw, k_raw, u_raw),
                queries,
                weights,
                heads,
                incoming,
                mixed,
                row_scale,
                branch,
                hidden_ffn,
                gate,
                up,
                product,
                (decay, query_decay, key_decay, slopes),
                (w_kv, w_quo, w_ffn),
            )
        )
    out_tokens = from_ring(residual)

    masked = to_ring(
        jnp.concatenate(
            [lax.dynamic_slice_in_dim(cotangent, (rank ^ j) * rows, rows, 0) for j in range(ranks)]
        )
    ) * live[:, None].astype(f32)
    grads = masked[:rows]
    back_ffn = masked.astype(bf16)
    totals = [None] * LAYERS

    def pieces(gradient):
        return [gradient[:, k * part : (k + 1) * part] for k in range(count)]

    running = []

    def tick(value):
        for job in running:
            if job.hops < hops:
                value = job.before(value)
                job.step()
        return value

    for level in reversed(range(LAYERS)):
        (
            x_att,
            x_ffn,
            hidden,
            (q_raw, k_raw, u_raw),
            queries,
            weights,
            heads,
            incoming,
            mixed,
            row_scale,
            branch,
            hidden_ffn,
            gate,
            up,
            product,
            (decay, query_decay, key_decay, slopes),
            (w_kv, w_quo, w_ffn),
        ) = stored[level]
        if back_ffn is None:
            back_ffn = head_gather(tick(grads.astype(bf16)))
        grad_product = dot_nt(back_ffn, w_ffn[2 * ffw :])
        grad_gate_up = jnp.concatenate([grad_product * up, grad_product * gate], axis=1).astype(bf16)
        grad_hidden = dot_nn(grad_gate_up, w_ffn[: 2 * ffw]).astype(bf16)
        branch_grad = head_scatter(tick(grad_hidden).reshape(ranks, rows, D))
        grad_ffn = jnp.concatenate(
            [dot_tn(grad_gate_up, hidden_ffn), dot_tn(product, back_ffn)], axis=0
        ).astype(bf16)
        s_ffn = Scatter(pieces(grad_ffn), count)
        s_ffn.step()
        running.append(s_ffn)
        grads = grads + norm_back(x_ffn, branch_grad)
        own_back = grads.astype(bf16)
        inner = jnp.sum(own_back.astype(f32) * branch, axis=1)
        back_att = head_gather(tick(own_back))
        inner = jnp.concatenate(head_gather_small(inner))
        grad_gated = dot_nt(back_att, w_quo[2 * att :])
        scale = row_scale[:, None]
        normed = mixed * scale
        gated = (normed * u_raw).astype(bf16)
        grad_u = (grad_gated * normed).astype(bf16)
        grad_mixed = (
            scale * (grad_gated * u_raw) - mixed * (scale * scale * scale * inner[:, None] / D)
        ).astype(bf16)
        state_grads = []
        for h in range(local_heads):
            gm = grad_mixed[:, h * HEAD_DIM : (h + 1) * HEAD_DIM]
            weighted = (queries[h].astype(f32) * query_decay[:, h : h + 1]).astype(bf16)
            state_grads.append(dot_tn(weighted, gm))
        outgoing = carried(
            jnp.stack(state_grads), group, count, free, slopes * capacity, False
        )
        grad_q, grad_k, grad_v = [], [], []
        for h in range(local_heads):
            cols = slice(h * HEAD_DIM, (h + 1) * HEAD_DIM)
            keys, values, decayed, _ = heads[h]
            gm = grad_mixed[:, cols]
            grad_scores = (dot_nt(gm, values) * decay[h]).astype(bf16)
            gq = dot_nn(grad_scores, keys) + query_decay[:, h : h + 1] * dot_nt(gm, incoming[h])
            gk = dot_tn(grad_scores, queries[h]) + key_decay[:, h : h + 1] * dot_nt(
                values, outgoing[h]
            )
            gv = dot_tn(weights[h], gm) + dot_nn(decayed, outgoing[h])
            grad_q.append(unrotate(gq, q_raw[:, cols], cosine, sine).astype(bf16))
            grad_k.append(unrotate(gk, k_raw[:, cols], cosine, sine).astype(bf16))
            grad_v.append(gv.astype(bf16))
        grad_qu = jnp.concatenate(grad_q + [grad_u], axis=1)
        grad_kv = jnp.concatenate(grad_k + grad_v, axis=1)
        grad_quo = jnp.concatenate([dot_tn(grad_qu, hidden), dot_tn(gated, back_att)], axis=0)
        s_quo = Scatter(pieces(grad_quo.astype(bf16)), count)
        s_quo.step()
        running.append(s_quo)
        grad_hidden = (dot_nn(grad_qu, w_quo[: 2 * att]) + dot_nn(grad_kv, w_kv)).astype(bf16)
        branch_grad = head_scatter(tick(grad_hidden).reshape(ranks, rows, D))
        s_kv = Scatter(pieces(dot_tn(grad_kv, hidden).astype(bf16)), count)
        s_kv.step()
        running.append(s_kv)
        grads = grads + norm_back(x_att, branch_grad)
        back_ffn = None
        totals[level] = (s_kv, s_quo, s_ffn)
    grad_tokens = from_ring(grads)
    totals = [[job.total() for job in jobs] for jobs in totals]

    squares = sum(jnp.sum(t * t) for jobs in totals for t in jobs)
    squares = jnp.full((8, 128), squares)
    for pairs in (NEAR, FAR):
        squares = squares + lax.ppermute(squares, "head", pairs)
    s = 1
    while s < count:
        squares = squares + lax.ppermute(squares, "dp", [(i, i ^ s) for i in range(count)])
        s *= 2
    grad_norm = jnp.sqrt(squares[0, 0])
    factor = jnp.minimum(1.0, 1.0 / (grad_norm + 1e-06))
    rate = 0.1 * math.sqrt(LAYERS * (5 * D * D + 3 * D * FF) / D)

    def update(weight, moment, average, gradient):
        clipped = gradient * factor
        new_moment = 0.9 * moment + clipped
        new_weight = weight - rate * (clipped + 0.9 * new_moment)
        new_average = 0.8 * average + 0.2 * new_weight
        return (new_moment, new_average, new_weight)

    def unflat(array, parts):
        return jnp.swapaxes(array.reshape(parts, -1, part), 1, 2)

    grad_qkvu = jnp.stack(
        [
            jnp.concatenate([unflat(quo[:att], 1), unflat(kv, 2), unflat(quo[att : 2 * att], 1)])
            for kv, quo, _ in totals
        ]
    )
    grad_out = jnp.stack([quo[2 * att :] for _, quo, _ in totals])
    grad_gu = jnp.stack([unflat(ffn[: 2 * ffw], 2) for _, _, ffn in totals])
    grad_down = jnp.stack([ffn[2 * ffw :] for _, _, ffn in totals])
    moment_qkvu, average_qkvu, weight_qkvu = update(w_qkvu, m_qkvu, e_qkvu, grad_qkvu)
    moment_out, average_out, weight_out = update(w_out, m_out, e_out, grad_out)
    moment_gu, average_gu, weight_gu = update(w_gu, m_gu, e_gu, grad_gu)
    moment_down, average_down, weight_down = update(w_down, m_down, e_down, grad_down)
    return (
        out_tokens,
        grad_tokens,
        grad_norm,
        moment_qkvu,
        moment_out,
        moment_gu,
        moment_down,
        average_qkvu,
        average_out,
        average_gu,
        average_down,
        weight_qkvu,
        weight_out,
        weight_gu,
        weight_down,
    )


def solution(mesh):
    rows = P(("dp", "head"), None)
    by_row = P(None, None, "dp", "head")
    by_column = P(None, "head", "dp")
    weights = (by_row, by_column, by_row, by_column)
    return jax.shard_map(
        per_device,
        mesh=mesh,
        in_specs=(rows, P("dp", None), P()) + weights * 3,
        out_specs=(rows, rows, P()) + weights * 3,
        check_vma=False,
    )
```

```python
import math

import jax
import jax.numpy as jnp
from jax import lax
from jax.experimental import pallas as pl
from jax.experimental.pallas import tpu as pltpu
from jax.sharding import PartitionSpec as P

D = 1024
HEADS = 8
HEAD_DIM = 128
FF = 2816
DEPTH = 24
LAYERS = 2
FIRST_LAYER = 21

epsilon = 1e-06
bf16 = jnp.bfloat16
f32 = jnp.float32


def dot_nn(a, b):
    return lax.dot_general(a, b, (((1,), (0,)), ((), ())), preferred_element_type=f32)


def dot_nt(a, b):
    return lax.dot_general(a, b, (((1,), (1,)), ((), ())), preferred_element_type=f32)


def dot_tn(a, b):
    return lax.dot_general(a, b, (((0,), (0,)), ((), ())), preferred_element_type=f32)


def ring_order(count):
    return list(range(0, count, 2)) + list(range(1, count, 2))[::-1]


def ring_pairs(count):
    order = ring_order(count)
    ahead = [(order[i], order[(i + 1) % count]) for i in range(count)]
    return ahead, [(b, a) for a, b in ahead]


def tie(value, *others):
    return lax.optimization_barrier((value,) + others)[0]


class Gather:
    def __init__(self, shard, count):
        self.pairs = ring_pairs(count)
        self.count = count
        self.hops = 0
        self.pieces = [shard] + [None] * (count - 1)
        self.moving = (shard, shard)

    def step(self):
        self.hops += 1
        k, count = self.hops, self.count
        ahead, behind = self.moving
        if k == count // 2:
            half = ahead.shape[0] // 2
            ahead, behind = ahead[:half], behind[half:]
        ahead = lax.ppermute(ahead, "dp", self.pairs[0])
        behind = lax.ppermute(behind, "dp", self.pairs[1])
        self.moving = (ahead, behind)
        if k == count // 2:
            self.pieces[k] = (ahead, behind)
        else:
            self.pieces[k], self.pieces[count - k] = ahead, behind

    def after(self, *values):
        self.moving = lax.optimization_barrier((*self.moving, *values))[:2]

    def before(self, value):
        return tie(value, *self.moving)

    def weight(self):
        while self.hops < self.count // 2:
            self.step()
        pieces, half = self.pieces, self.count // 2
        if pieces[0].shape[1] % 128:
            pieces = [jnp.concatenate(p, axis=0) if k == half else p for k, p in enumerate(pieces)]
            return Weight([jnp.concatenate(pieces, axis=1)], [(0, 0)])
        arrays, places = [], []
        for k, piece in enumerate(pieces):
            column = k * pieces[0].shape[1]
            if k == half:
                arrays += list(piece)
                places += [(0, column), (piece[0].shape[0], column)]
            else:
                arrays.append(piece)
                places.append((0, column))
        return Weight(arrays, places)


def owner_of(group, k, count):
    here = jnp.where(group % 2 == 0, group // 2, count - 1 - group // 2)
    place = (here - k + count) % count
    return jnp.where(place < count // 2, 2 * place, 2 * (count - 1 - place) + 1)


class Weight:
    def __init__(self, arrays, places=None):
        self.arrays, self.places = arrays, places

    def scratch(self):
        count = len(self.arrays) if self.places else self.arrays[0].shape[0]
        return [pltpu.SemaphoreType.DMA((count,))]

    def copies(self, refs, whole, arrived, low, high, info=None):
        out = []
        if self.places is None:
            count, _, width = refs[0].shape
            for k in range(count):
                out.append(
                    pltpu.make_async_copy(
                        refs[0].at[owner_of(info[0], k, count), pl.ds(low, high - low), :],
                        whole.at[pl.ds(low, high - low), pl.ds(k * width, width)],
                        arrived.at[k],
                    )
                )
            return out
        for i, (ref, (row, column)) in enumerate(zip(refs, self.places)):
            first, after = max(low, row), min(high, row + ref.shape[0])
            if first < after:
                out.append(
                    pltpu.make_async_copy(
                        ref.at[pl.ds(first - row, after - first), :],
                        whole.at[pl.ds(first, after - first), pl.ds(column, ref.shape[1])],
                        arrived.at[i],
                    )
                )
        return out


def piece_shapes(rows, count):
    part = D // count
    if part % 128:
        return [((rows, D), 0, 0)]
    out = []
    for k in range(count):
        if k == count // 2:
            out += [((rows // 2, part), 0, k * part), ((rows // 2, part), rows // 2, k * part)]
        else:
            out.append(((rows, part), 0, k * part))
    return out


def store_pieces(refs, shapes, value, low):
    for ref, (shape, row, column) in zip(refs, shapes):
        first, after = max(low, row), min(low + value.shape[0], row + shape[0])
        if first < after:
            ref[first - row : after - row, :] = value[
                first - low : after - low, column : column + shape[1]
            ].astype(ref.dtype)


def pieces_of(outputs, count):
    if len(outputs) == 1:
        whole, part, half = outputs[0], D // count, outputs[0].shape[0] // 2
        pieces = [whole[:, k * part : (k + 1) * part] for k in range(count)]
        middle = pieces[count // 2]
        pieces[count // 2] = (middle[:half], middle[half:])
        return pieces
    middle = count // 2
    return outputs[:middle] + [tuple(outputs[middle : middle + 2])] + outputs[middle + 2 :]


class Scatter:
    def __init__(self, pieces, count):
        self.pairs = ring_pairs(count)
        self.count = count
        self.hops = 0
        self.pieces = pieces
        self.moving = pieces[count // 2][::-1]

    def step(self):
        self.hops += 1
        k, count = self.count // 2 - self.hops, self.count
        ahead = lax.ppermute(self.moving[0], "dp", self.pairs[0])
        behind = lax.ppermute(self.moving[1], "dp", self.pairs[1])
        if k:
            mine = (self.pieces[count - k], self.pieces[k])
            self.moving = launch(
                add_on_the_way,
                [(piece.shape, bf16) for piece in mine],
                arrays=(*mine, ahead, behind),
            )
        else:
            self.moving = (ahead, behind)

    def after(self, *values):
        self.moving = lax.optimization_barrier((*self.moving, *values))[:2]

    def before(self, value):
        return tie(value, *self.moving)

    def parts_of_total(self):
        while self.hops < self.count // 2:
            self.step()
        return [self.pieces[0], *self.moving]


def add_on_the_way(_, arrays, __, outs, ___):
    for i in range(2):
        mine, moving, out = arrays[i], arrays[2 + i], outs[i]
        rows, half = mine.shape[0], moving.shape[0]
        first = rows - half if i == 0 else 0
        if half < rows:
            rest = slice(0, half) if i == 0 else slice(half, rows)
            out[rest, :] = mine[rest, :]
        at = slice(first, first + half)
        out[at, :] = (mine[at, :].astype(f32) + moving[...].astype(f32)).astype(bf16)


def launch(body, outputs, scalars=(), arrays=(), parts=(), scratch=(), pinned=True):
    counts = [len(scalars), len(arrays), len(parts), len(outputs), len(scratch)]

    def kernel(*refs):
        groups, at = [], 0
        for size in counts:
            groups.append(refs[at : at + size])
            at += size
        body(*groups)

    spaces = (
        [pltpu.SMEM] * len(scalars) + [pltpu.VMEM] * len(arrays) + [pltpu.HBM] * len(parts)
    )
    return pl.pallas_call(
        kernel,
        out_shape=[
            (pltpu.VMEM if pinned else jax.ShapeDtypeStruct)(shape, kind) for shape, kind in outputs
        ],
        in_specs=[pl.BlockSpec(memory_space=space) for space in spaces],
        out_specs=[pl.BlockSpec(memory_space=pltpu.VMEM)] * len(outputs),
        scratch_shapes=list(scratch),
        compiler_params=pltpu.CompilerParams(vmem_limit_bytes=16 * 1024 * 1024),
        name=body.__name__,
    )(*scalars, *arrays, *parts)


NEAR = [(0, 1), (1, 0), (2, 3), (3, 2)]
FAR = [(0, 2), (2, 0), (1, 3), (3, 1)]
CROSS = [(0, 3), (3, 0), (1, 2), (2, 1)]


def head_gather(block):
    far = lax.ppermute(block, "head", FAR)
    near = lax.ppermute(block, "head", NEAR)
    cross = lax.ppermute(far, "head", NEAR)
    return [block, near, far, cross]


def head_gather_small(block):
    far = lax.ppermute(block, "head", FAR)
    near = lax.ppermute(block, "head", NEAR)
    cross = lax.ppermute(block, "head", CROSS)
    return [block, near, far, cross]


def head_scatter(blocks):
    near = lax.ppermute(blocks[1], "head", NEAR)
    cross = lax.ppermute(blocks[3], "head", NEAR)
    to_far = (blocks[2].astype(f32) + cross.astype(f32)).astype(bf16)
    far = lax.ppermute(to_far, "head", FAR)
    return [blocks[0], near, far]


def row_scale_of(values):
    return lax.rsqrt(jnp.mean(values * values, axis=-1, keepdims=True) + epsilon)


def norm_back(values, grads):
    factor = row_scale_of(values)
    inner = jnp.mean(values * grads, axis=-1, keepdims=True)
    return factor * grads - values * (factor * factor * factor) * inner


def silu(v):
    return v * jax.nn.sigmoid(v)


def segment_of(places, seq_ends):
    return jnp.sum((places[..., None] >= seq_ends).astype(jnp.int32), axis=-1, dtype=jnp.int32)


def sequence_ends(info):
    ends, end = [], 0
    for i in range(2, info.shape[0]):
        end = end + info[i]
        ends.append(end)
    return ends


def group_layout(info, shape, dim, rows):
    index = lax.broadcasted_iota(jnp.int32, shape, dim)
    local = ((index // rows) ^ info[1]) * rows + index % rows
    place = local + info[0] * (4 * rows)
    segment = jnp.zeros(shape, jnp.int32)
    for end in sequence_ends(info):
        segment = segment + jnp.where(place >= end, 1, 0)
    return local.astype(f32), place, segment


def segment_at(info, place):
    segment = 0
    for end in sequence_ends(info):
        segment = segment + jnp.where(place >= end, 1, 0)
    return segment


def slope_of(table, level, h, local_heads):
    row = level * local_heads + h
    return table[row : row + 1, 127:128]


def query_decays(info, table, level, local_heads, rows):
    position, _, segment = group_layout(info, (4 * rows, 1), 0, rows)
    seqs = info.shape[0] - 2
    inward = (segment == segment_at(info, info[0] * (4 * rows) - 1)) & (segment < seqs)
    return [
        jnp.where(inward, jnp.exp(-slope_of(table, level, h, local_heads) * (position + 1.0)), 0.0)
        for h in range(local_heads)
    ]


def key_decays(info, table, level, local_heads, rows):
    position, _, segment = group_layout(info, (4 * rows, 1), 0, rows)
    seqs, size = info.shape[0] - 2, 4 * rows
    outward = (segment == segment_at(info, info[0] * size + (size - 1))) & (segment < seqs)
    return [
        jnp.where(
            outward,
            jnp.exp(-slope_of(table, level, h, local_heads) * (size - 1.0 - position)),
            0.0,
        )
        for h in range(local_heads)
    ]


def decay_parts(info, rows):
    size, seqs = 4 * rows, info.shape[0] - 2
    row_place, _, row_segment = group_layout(info, (size, 1), 0, rows)
    column_place, _, column_segment = group_layout(info, (1, size), 1, rows)
    apart = row_place - column_place
    allowed = (apart >= 0.0) & (row_segment == column_segment) & (row_segment < seqs)
    return jnp.maximum(apart, 0.0), allowed


def ring_columns(info, k, count, part):
    if part % 128:
        return slice(k * part, (k + 1) * part)
    return pl.ds(pl.multiple_of(owner_of(info[0], k, count) * part, 128), part)


def set_out(count, local_heads):
    def body(scalars, arrays, _, outs, __):
        info, tokens = scalars[0], arrays[0]
        x, hidden, cosine, sine, table = outs
        rows, part = tokens.shape[0], D // count
        for k in range(count):
            x[:, k * part : (k + 1) * part] = tokens[:, ring_columns(info, k, count, part)]
        values = x[...]
        hidden[...] = (values * row_scale_of(values)).astype(bf16)
        size = 4 * rows
        _, place, segment = group_layout(info, (size, 1), 0, rows)
        begins, end = jnp.zeros((size, 1), jnp.int32), 0
        for i in range(info.shape[0] - 2):
            begins = begins + jnp.where(segment == i, end, 0)
            end = end + info[2 + i]
        lane = lax.broadcasted_iota(jnp.int32, (1, HEAD_DIM), 1).astype(f32)
        frequency = jnp.exp(-math.log(10000.0) * lane / HEAD_DIM)
        angles = (place - begins).astype(f32) * frequency
        cosine[...] = jnp.cos(angles)
        sine[...] = jnp.sin(angles)
        row = lax.broadcasted_iota(jnp.int32, (8, 128), 0)
        lane = lax.broadcasted_iota(jnp.int32, (8, 128), 1)
        head = info[1] * local_heads + row % local_heads
        depth = (FIRST_LAYER + row // local_heads).astype(f32)
        base = jnp.exp(-8.0 * math.log(2.0) * (head + 1).astype(f32) / HEADS)
        slope = base * (1.0 - depth / (DEPTH - 1.0) + 1e-05)
        pairs = count // 2
        pair = info[0] // 2
        first = 2 * pair
        before = first * 0 + 2 * ((lane - 1) ^ pair)
        after = 2 * ((lane - pairs) ^ pair)
        low = jnp.where(lane < 2, first + lane, jnp.where(lane <= pairs, before + 2, first + 2))
        high = jnp.where(lane < 2, first + lane + 1, jnp.where(lane <= pairs, first, after))
        broken = jnp.where(high < low, 1, 0)
        for g in range(count):
            begin, last = segment_at(info, g * size), segment_at(info, (g + 1) * size - 1)
            joined = jnp.where(begin == last, 1, 0) * jnp.where(last < info.shape[0] - 2, 1, 0)
            broken = broken + jnp.where((low <= g) & (g < high), 1 - joined, 0)
        steps = jnp.maximum(high - low, 0).astype(f32)
        factors = jnp.where(broken == 0, jnp.exp(-slope * size * steps), 0.0)
        table[...] = jnp.where(lane == 127, slope, factors)

    return body


def take_cotangent(count):
    def body(scalars, arrays, _, outs, __):
        info, cotangent = scalars[0], arrays[0]
        rows, part = cotangent.shape[0] // 4, D // count
        _, _, segment = group_layout(info, (4 * rows, 1), 0, rows)
        live = jnp.where(segment < info.shape[0] - 2, 1.0, 0.0)
        for j in range(4):
            at = pl.ds(pl.multiple_of((info[1] ^ j) * rows, rows), rows)
            for k in range(count):
                columns = slice(k * part, (k + 1) * part)
                value = cotangent[at, ring_columns(info, k, count, part)]
                value = value * live[j * rows : (j + 1) * rows, :]
                if j == 0:
                    outs[0][:, columns] = value
                outs[1 + j][:, columns] = value.astype(bf16)

    return body


def store_natural(ref, info, value, count):
    part = D // count
    for k in range(count):
        ref[:, ring_columns(info, k, count, part)] = value[:, k * part : (k + 1) * part]


def stacked(refs):
    return jnp.concatenate([ref[...] for ref in refs], axis=0)


def rotated(active, cosine, sine):
    return jnp.concatenate([active * cosine, active * sine], axis=1).astype(bf16)


def head_columns(h):
    return slice(h * HEAD_DIM, (h + 1) * HEAD_DIM)


def row_of_sums(values):
    ones = jnp.ones((8, values.shape[1]), f32)
    return lax.dot_general(
        ones, values, (((1,), (1,)), ((), ())), precision=lax.Precision.HIGHEST,
        preferred_element_type=f32,
    )


def column_of(row):
    size = row.shape[1]
    same = lax.broadcasted_iota(jnp.int32, (size, size), 0) == lax.broadcasted_iota(
        jnp.int32, (size, size), 1
    )
    return jnp.sum(jnp.where(same, jnp.broadcast_to(row, (size, size)), 0.0), axis=1, keepdims=True)


def summed_column(refs, j, rows):
    row = sum(
        ref[0:1, (j ^ mask) * rows : (j ^ mask) * rows + rows] for mask, ref in enumerate(refs)
    )
    return column_of(row)


def prepare_attention(level):
    def prepare(_, arrays, __, outs, ___):
        w_qkvu, w_out = arrays
        size = w_out.shape[1]
        for i, which in enumerate((1, 2, 0, 3)):
            outs[0][i * size : (i + 1) * size, :] = jnp.transpose(w_qkvu[level, which]).astype(bf16)
        outs[0][4 * size :, :] = w_out[level].astype(bf16)

    return prepare


def prepare_unit(level):
    def prepare(_, arrays, __, outs, ___):
        w_gu, w_down = arrays
        size = w_down.shape[1]
        for i in range(2):
            outs[0][i * size : (i + 1) * size, :] = w_gu[level, i].astype(bf16)
        outs[0][2 * size :, :] = w_down[level].astype(bf16)

    return prepare


def keys_values(weight, rows, level):
    def body(scalars, arrays, parts, outs, scratch):
        (info,) = scalars
        cosine, sine, table = arrays[4:]
        k_raw, keys, values, states, whole = outs
        heads = states.shape[0]
        att = k_raw.shape[1]
        copies = weight.copies(parts, whole, scratch[0], 0, 2 * att, info)
        later = weight.copies(parts, whole, scratch[1], 2 * att, 5 * att, info)
        for copy in copies + later:
            copy.start()
        decays = key_decays(info, table, level, heads, rows)
        hidden = stacked(arrays[:4])
        for copy in copies:
            copy.wait()
        for h in range(heads):
            cols = head_columns(h)
            raw = dot_nt(hidden, whole[h * HEAD_DIM : (h + 1) * HEAD_DIM, :])
            k_raw[:, cols] = raw
            key = rotated(silu(raw), cosine[...], sine[...])
            keys[h] = key
            at = att + h * HEAD_DIM
            value = dot_nt(hidden, whole[at : at + HEAD_DIM, :]).astype(bf16)
            values[:, cols] = value
            decayed = (key.astype(f32) * decays[h]).astype(bf16)
            states[h] = dot_tn(decayed, value).astype(bf16)
        for copy in later:
            copy.wait()

    return body


def pair_states(forward, level):
    def body(scalars, arrays, _, outs, __):
        (info,) = scalars
        table, own, other = arrays
        heads = own.shape[0]
        even = jnp.where(info[0] % 2 == 0, 1.0, 0.0)
        for h in range(heads):
            row = level * heads + h
            a, b = own[h].astype(f32), other[h].astype(f32)
            low, high = even * a + (1.0 - even) * b, even * b + (1.0 - even) * a
            if forward:
                both = table[row : row + 1, 1:2] * low + high
            else:
                both = low + table[row : row + 1, 0:1] * high
            outs[0][h] = both.astype(bf16)

    return body


def carried_state(info, table, level, own, other, moved, h, forward):
    row, pairs = level * own.shape[0] + h, len(moved)
    even = jnp.where(info[0] % 2 == 0, 1.0, 0.0)
    total = jnp.zeros(own.shape[1:], f32)
    for i, ref in enumerate(moved):
        at = 2 + i + (0 if forward else pairs)
        total = total + table[row : row + 1, at : at + 1] * ref[h].astype(f32)
    if forward:
        step = table[row : row + 1, 0:1] * total + other[h].astype(f32)
        total = even * total + (1.0 - even) * step
    else:
        step = table[row : row + 1, 1:2] * total + other[h].astype(f32)
        total = even * step + (1.0 - even) * total
    return total.astype(bf16)


def within_group(rows, level):
    def body(scalars, arrays, parts, outs, scratch):
        (info,) = scalars
        cosine, sine, keys, values, whole, table = arrays[4:]
        q_raw, u_raw, queries, weights, within = outs
        heads = weights.shape[0]
        att = q_raw.shape[1]
        apart, allowed = decay_parts(info, rows)
        hidden = stacked(arrays[:4])
        for h in range(heads):
            cols = head_columns(h)
            at = 2 * att + h * HEAD_DIM
            raw = dot_nt(hidden, whole[at : at + HEAD_DIM, :])
            q_raw[:, cols] = raw
            query = rotated(silu(raw), cosine[...], sine[...])
            queries[h] = query
            decay = jnp.where(allowed, jnp.exp(-slope_of(table, level, h, heads) * apart), 0.0)
            score = (dot_nt(query, keys[h]) * decay).astype(bf16)
            weights[h] = score
            within[:, cols] = dot_nn(score, values[:, cols])
        u_raw[...] = dot_nt(hidden, whole[3 * att : 4 * att, :])

    return body


def mix(rows, level):
    def body(scalars, arrays, parts, outs, scratch):
        (info,) = scalars
        whole, table, queries, within, u_raw, own, other = arrays[:7]
        moved = arrays[7:]
        mixed, incoming, squares = outs[:3]
        att, heads = mixed.shape[1], own.shape[0]
        decays = query_decays(info, table, level, heads, rows)
        gated = []
        for h in range(heads):
            cols = head_columns(h)
            state = carried_state(info, table, level, own, other, moved, h, True)
            incoming[h] = state
            value = within[:, cols] + decays[h] * dot_nn(queries[h], state)
            mixed[:, cols] = value
            gated.append((value * u_raw[:, cols]).astype(bf16))
        gated = jnp.concatenate(gated, axis=1)
        squares[...] = row_of_sums(mixed[...] * mixed[...])
        for j, ref in enumerate(outs[3:]):
            ref[...] = dot_nn(gated[j * rows : (j + 1) * rows, :], whole[4 * att :, :]).astype(bf16)

    return body


def add_attention(_, arrays, __, outs, ___):
    x, first, near, far = arrays[:4]
    x_out, branch, hidden = outs
    scale = lax.rsqrt(summed_column(arrays[4:], 0, x.shape[0]) / D + epsilon)
    total = first[...].astype(f32) + near[...].astype(f32) + far[...].astype(f32)
    branch[...] = total
    value = x[...] + total * scale
    x_out[...] = value
    hidden[...] = (value * row_scale_of(value)).astype(bf16)


def add_unit(count):
    def body(scalars, arrays, __, outs, ___):
        x, first, near, far = arrays
        value = x[...] + (first[...].astype(f32) + near[...].astype(f32) + far[...].astype(f32))
        if len(outs) > 1:
            outs[0][...] = value
            outs[1][...] = (value * row_scale_of(value)).astype(bf16)
        else:
            store_natural(outs[0], scalars[0], value, count)

    return body


def gated_unit(weight, rows):
    def body(_, arrays, parts, outs, scratch):
        gate, up, product, whole = outs[:4]
        ffw = gate.shape[1]
        copies = [
            weight.copies(parts, whole, scratch[i], i * ffw, (i + 1) * ffw) for i in range(3)
        ]
        for copy in sum(copies, []):
            copy.start()
        hidden = stacked(arrays)
        for copy in copies[0]:
            copy.wait()
        a = dot_nt(hidden, whole[:ffw, :])
        for copy in copies[1]:
            copy.wait()
        b = dot_nt(hidden, whole[ffw : 2 * ffw, :])
        gate[...] = a.astype(bf16)
        up[...] = b.astype(bf16)
        value = (a * b).astype(bf16)
        product[...] = value
        for copy in copies[2]:
            copy.wait()
        for j, ref in enumerate(outs[4:]):
            ref[...] = dot_nn(value[j * rows : (j + 1) * rows, :], whole[2 * ffw :, :]).astype(bf16)

    return body


def unit_back(rows):
    def body(_, arrays, parts, outs, scratch):
        gate, up, whole = arrays[4:]
        grad_gate, grad_up = outs[:2]
        ffw = gate.shape[1]
        back = stacked(arrays[:4])
        grad = dot_nt(back, whole[2 * ffw :, :])
        a = (grad * up[...].astype(f32)).astype(bf16)
        b = (grad * gate[...].astype(f32)).astype(bf16)
        grad_gate[...] = a
        grad_up[...] = b
        for j, ref in enumerate(outs[2:]):
            block = slice(j * rows, (j + 1) * rows)
            ref[...] = (
                dot_nn(a[block, :], whole[:ffw, :]) + dot_nn(b[block, :], whole[ffw : 2 * ffw, :])
            ).astype(bf16)

    return body


def unit_weights(shapes):
    def body(_, arrays, __, outs, ___):
        hidden, back = stacked(arrays[3:7]), stacked(arrays[7:])
        ffw = arrays[0].shape[1]
        for i, right in enumerate((hidden, hidden, back)):
            store_pieces(outs, shapes, dot_tn(arrays[i][...], right), i * ffw)

    return body


def attention_weights(shapes, lefts):
    def body(_, arrays, __, outs, ___):
        rights = [stacked(arrays[-8:-4]), stacked(arrays[-4:])]
        at = 0
        for i, which in enumerate(lefts):
            grad = dot_tn(arrays[i][...], rights[which])
            store_pieces(outs, shapes, grad, at)
            at += grad.shape[0]

    return body


def back_through_norm(x, grads, arrays):
    first, near, far = arrays
    incoming = first[...].astype(f32) + near[...].astype(f32) + far[...].astype(f32)
    return grads[...] + norm_back(x[...], incoming)


def unit_norm_back(_, arrays, __, outs, ___):
    x, grads, branch = arrays[:3]
    new, own, inner = outs
    value = back_through_norm(x, grads, arrays[3:])
    new[...] = value
    rounded = value.astype(bf16)
    own[...] = rounded
    inner[...] = row_of_sums(rounded.astype(f32) * branch[...])


def attention_norm_back(count):
    def body(scalars, arrays, __, outs, ___):
        x, grads = arrays[:2]
        value = back_through_norm(x, grads, arrays[2:])
        if len(outs) > 1:
            outs[0][...] = value
            outs[1][...] = value.astype(bf16)
        else:
            store_natural(outs[0], scalars[0], value, count)

    return body


def mixed_back(rows, level):
    def body(scalars, arrays, parts, outs, scratch):
        (info,) = scalars
        back_refs, square_refs, inner_refs = arrays[:4], arrays[4:8], arrays[8:12]
        mixed, u_raw, queries, whole, table = arrays[12:]
        gated, grad_u, grad_mixed, states = outs
        att, heads = mixed.shape[1], states.shape[0]
        decays = query_decays(info, table, level, heads, rows)
        scale = jnp.concatenate(
            [
                lax.rsqrt(summed_column(square_refs, j, rows) / D + epsilon) for j in range(4)
            ],
            axis=0,
        )
        inner = jnp.concatenate([column_of(ref[0:1, :]) for ref in inner_refs], axis=0)
        factor = scale * scale * inner / D
        back = stacked(back_refs)
        grad_gated = dot_nt(back, whole[4 * att :, :])
        value, u = mixed[...], u_raw[...]
        normed = value * scale
        gated[...] = (normed * u).astype(bf16)
        grad_u[...] = (grad_gated * normed).astype(bf16)
        grad = (scale * (grad_gated * u) - value * (scale * factor)).astype(bf16)
        grad_mixed[...] = grad
        for h in range(heads):
            weighted = (queries[h].astype(f32) * decays[h]).astype(bf16)
            states[h] = dot_tn(weighted, grad[:, head_columns(h)]).astype(bf16)

    return body


def unrotated(grad, raw, cosine, sine):
    active = grad[:, :HEAD_DIM] * cosine + grad[:, HEAD_DIM:] * sine
    sigma = jax.nn.sigmoid(raw)
    return active * (sigma * (1.0 + raw * (1.0 - sigma)))


def within_back(rows, level):
    def body(scalars, arrays, parts, outs, scratch):
        (info,) = scalars
        grad_mixed, grad_u, values, keys, queries, weights, incoming, q_raw = arrays[:8]
        cosine, sine, whole, table = arrays[8:]
        grad_q, key_part, value_part, hidden_part = outs
        att, heads = q_raw.shape[1], weights.shape[0]
        apart, allowed = decay_parts(info, rows)
        decays = query_decays(info, table, level, heads, rows)
        for h in range(heads):
            cols = head_columns(h)
            grad = grad_mixed[:, cols]
            decay = jnp.where(allowed, jnp.exp(-slope_of(table, level, h, heads) * apart), 0.0)
            scores = (dot_nt(grad, values[:, cols]) * decay).astype(bf16)
            to_query = dot_nn(scores, keys[h]) + decays[h] * dot_nt(grad, incoming[h])
            grad_q[:, cols] = unrotated(
                to_query, q_raw[:, cols], cosine[...], sine[...]
            ).astype(bf16)
            key_part[h] = dot_tn(scores, queries[h])
            value_part[:, cols] = dot_tn(weights[h], grad)
        hidden_part[...] = dot_nn(grad_q[...], whole[2 * att : 3 * att, :]) + dot_nn(
            grad_u[...], whole[3 * att : 4 * att, :]
        )

    return body


def keys_back(rows, level):
    def body(scalars, arrays, parts, outs, scratch):
        (info,) = scalars
        key_part, value_part, hidden_part, k_raw, keys, values, cosine, sine = arrays[:8]
        whole, table, own, other = arrays[8:12]
        moved = arrays[12:]
        grad_k, grad_v = outs[:2]
        att, heads = k_raw.shape[1], own.shape[0]
        decays = key_decays(info, table, level, heads, rows)
        for h in range(heads):
            cols = head_columns(h)
            state = carried_state(info, table, level, own, other, moved, h, False)
            key, value = keys[h], values[:, cols]
            to_key = key_part[h] + decays[h] * dot_nt(value, state)
            decayed = (key.astype(f32) * decays[h]).astype(bf16)
            grad_v[:, cols] = (value_part[:, cols] + dot_nn(decayed, state)).astype(bf16)
            grad_k[:, cols] = unrotated(
                to_key, k_raw[:, cols], cosine[...], sine[...]
            ).astype(bf16)
        for j, ref in enumerate(outs[2:]):
            block = slice(j * rows, (j + 1) * rows)
            ref[...] = (
                hidden_part[block, :]
                + dot_nn(grad_k[block, :], whole[:att, :])
                + dot_nn(grad_v[block, :], whole[att : 2 * att, :])
            ).astype(bf16)

    return body


def finish(_, arrays, __, outs, ___):
    total = arrays[0][...].astype(f32)
    for ref in arrays[1:]:
        total = total + ref[...].astype(f32)
    outs[0][...] = total
    squares = total * total
    outs[1][...] = jnp.sum(squares.reshape(-1, 8, squares.shape[1]), axis=0)


def step_sizes(squares):
    norm = jnp.sqrt(jnp.full((8, 128), jnp.sum(squares[...]), f32))
    return norm, jnp.minimum(1.0, 1.0 / (norm + 1e-06))[0:1, 0:1]


def renew(refs, outs, at, gradient, factor):
    weight, moment, average = (ref[at] for ref in refs)
    rate = 0.1 * math.sqrt(LAYERS * (5 * D * D + 3 * D * FF) / D)
    clipped = gradient * factor
    new_moment = 0.9 * moment + clipped
    new_weight = weight - rate * (clipped + 0.9 * new_moment)
    outs[0][at] = new_moment
    outs[1][at] = 0.8 * average + 0.2 * new_weight
    outs[2][at] = new_weight


def renew_attention(_, arrays, __, outs, ___):
    norm, factor = step_sizes(arrays[0])
    size = arrays[4].shape[1]
    for level in range(LAYERS):
        total = arrays[7 + level]
        for i, which in enumerate((1, 2, 0, 3)):
            gradient = jnp.transpose(total[i * size : (i + 1) * size, :])
            renew(arrays[1:4], outs[:3], (level, which), gradient, factor)
        renew(arrays[4:7], outs[3:6], (level,), total[4 * size :, :], factor)
    outs[6][...] = norm


def renew_unit(_, arrays, __, outs, ___):
    _, factor = step_sizes(arrays[0])
    size = arrays[4].shape[1]
    for level in range(LAYERS):
        total = arrays[7 + level]
        for i in range(2):
            gradient = total[i * size : (i + 1) * size, :]
            renew(arrays[1:4], outs[:3], (level, i), gradient, factor)
        renew(arrays[4:7], outs[3:6], (level,), total[2 * size :, :], factor)


def exchanged(states, info, table, level, count, forward, hop):
    other = lax.ppermute(states, "dp", [(i, i ^ 1) for i in range(count)])
    other = hop(other)
    (both,) = launch(
        pair_states(forward, level), [(states.shape, bf16)], (info,), (table, states, other)
    )
    return other, [
        lax.ppermute(both, "dp", [(i, i ^ (2 * s)) for i in range(count)])
        for s in range(1, count // 2)
    ]


def per_device(
    tokens,
    cotangent,
    lengths,
    w_qkvu,
    w_out,
    w_gu,
    w_down,
    m_qkvu,
    m_out,
    m_gu,
    m_down,
    e_qkvu,
    e_out,
    e_gu,
    e_down,
):
    rows = tokens.shape[0]
    count = lax.axis_size("dp")
    ranks = lax.axis_size("head")
    group = lax.axis_index("dp")
    rank = lax.axis_index("head")
    capacity = rows * ranks
    local_heads = HEADS // ranks
    att = local_heads * HEAD_DIM
    ffw = FF // ranks
    part = D // count

    order = ring_order(count)
    place = [order.index(i) for i in range(count)]
    my_place = jnp.array(place, jnp.int32)[group]
    owners = [jnp.array(order, jnp.int32)[(my_place - k) % count] for k in range(count)]
    sources = [(my_place - place[c]) % count for c in range(count)]

    def to_ring(array):
        return jnp.concatenate(
            [lax.dynamic_slice_in_dim(array, owners[k] * part, part, 1) for k in range(count)], axis=1
        )

    def from_ring(array):
        return jnp.concatenate(
            [lax.dynamic_slice_in_dim(array, sources[c] * part, part, 1) for c in range(count)], axis=1
        )

    hops = count // 2
    aligned = part % 128 == 0
    g_in, m_in, e_in = (jnp.swapaxes(a, 2, 3) for a in (w_gu, m_gu, e_gu))
    (shard,) = launch(
        prepare_attention(0), [((5 * att, part), bf16)], arrays=(w_qkvu, w_out), pinned=False
    )
    g_first = Gather(shard, count)
    g_first.step()
    info = jnp.concatenate([jnp.stack([group, rank]).astype(jnp.int32), lengths])
    x_att, own, cosine, sine, table = launch(
        set_out(count, local_heads),
        [
            ((rows, D), f32),
            ((rows, D), bf16),
            ((capacity, HEAD_DIM), f32),
            ((capacity, HEAD_DIM), f32),
            ((8, 128), f32),
        ],
        (info,),
        (tokens if aligned else to_ring(tokens),),
    )
    g_first.after(own)
    g_first.step()
    hidden = head_gather(own)
    g_first.after(*hidden)
    while g_first.hops < hops:
        g_first.step()
    later = []
    for level in range(1, LAYERS):
        (shard,) = launch(
            prepare_attention(level),
            [((5 * att, part), bf16)],
            arrays=(w_qkvu, w_out),
            pinned=False,
        )
        later.append(lax.all_gather(tie(shard, *g_first.moving), "dp", axis=0))
    ring = []
    for level in range(LAYERS):
        (shard,) = launch(prepare_unit(level), [((3 * ffw, part), bf16)], arrays=(g_in, w_down), pinned=False)
        ring.append(Gather(shard, count))

    def hop(value):
        for job in ring:
            if job.hops < hops:
                value = job.before(value)
                job.step()
                break
        return value

    def by_index(array):
        if part % 128 == 0:
            return Weight([array])
        parts = [lax.dynamic_index_in_dim(array, owners[k], 0, False) for k in range(count)]
        return Weight([jnp.concatenate(parts, axis=1)], [(0, 0)])

    block_out = [((rows, D), bf16)] * ranks
    row_out = ((rows, D), f32)
    width_f32 = ((capacity, att), f32)
    width_bf16 = ((capacity, att), bf16)
    pair_bf16 = ((local_heads, capacity, 2 * HEAD_DIM), bf16)
    state_bf16 = ((local_heads, 2 * HEAD_DIM, HEAD_DIM), bf16)
    unit_bf16 = ((capacity, ffw), bf16)

    w_parts = g_first.weight()
    stored = []
    for level in range(LAYERS):
        if level == 0:
            ring[0].after(*g_first.moving)
            ring[0].step()
        else:
            hidden = head_gather(hop(own))
            w_parts = by_index(later[level - 1])
        k_raw, keys, values, states, w_att = launch(
            keys_values(w_parts, rows, level),
            [width_f32, pair_bf16, width_bf16, state_bf16, ((5 * att, D), bf16)],
            (info,),
            (*hidden, cosine, sine, table),
            w_parts.arrays,
            w_parts.scratch() * 2,
        )
        other, moved = exchanged(states, info, table, level, count, True, hop)
        q_raw, u_raw, queries, weights, within = launch(
            within_group(rows, level),
            [
                width_f32,
                width_f32,
                pair_bf16,
                ((local_heads, capacity, capacity), bf16),
                width_f32,
            ],
            (info,),
            (*hidden, cosine, sine, keys, values, w_att, table),
        )
        mixed, incoming, squares, *partial = launch(
            mix(rows, level),
            [width_f32, state_bf16, ((8, capacity), f32)] + block_out,
            (info,),
            (w_att, table, queries, within, u_raw, states, other, *moved),
        )
        partial[3] = hop(partial[3])
        squares = head_gather_small(squares)
        first = head_scatter(partial)
        x_ffn, branch, own = launch(
            add_attention,
            [row_out, row_out, ((rows, D), bf16)],
            arrays=(x_att, *first, *squares),
        )
        hidden_ffn = head_gather(hop(own))
        w_parts = ring[level].weight()
        if level + 1 < LAYERS and ring[level + 1].hops == 0:
            ring[level + 1].after(*ring[level].moving)
            ring[level + 1].step()
        gate, up, product, w_ffn, *partial = launch(
            gated_unit(w_parts, rows),
            [unit_bf16] * 3 + [((3 * ffw, D), bf16)] + block_out,
            (),
            hidden_ffn,
            w_parts.arrays,
            w_parts.scratch() * 3,
        )
        partial[3] = hop(partial[3])
        first = head_scatter(partial)
        last = level + 1 == LAYERS
        outputs = launch(
            add_unit(count),
            [row_out] + [((rows, D), bf16)] * (not last),
            (info,),
            (x_ffn, *first),
            pinned=not last,
        )
        stored.append(
            (
                (x_att, x_ffn, branch),
                (hidden, hidden_ffn, squares),
                (q_raw, k_raw, u_raw),
                (queries, keys, values, weights, incoming, mixed),
                (gate, up, product),
                (w_att, w_ffn),
            )
        )
        x_att, own = outputs[0], outputs[-1]
    out_tokens = x_att if aligned else from_ring(x_att)

    grads, *back_ffn = launch(
        take_cotangent(count),
        [row_out] + block_out,
        (info,),
        (cotangent if aligned else to_ring(cotangent),),
    )

    def tick(value, *jobs):
        for job in jobs:
            if job is not None and job.hops < hops:
                value = job.before(value)
                job.step()
        return value

    def scatter(body, rows_out, arrays):
        shapes = piece_shapes(rows_out, count)
        outputs = launch(body(shapes), [(shape, bf16) for shape, _, _ in shapes], arrays=arrays, pinned=False)
        job = Scatter(pieces_of(list(outputs), count), count)
        job.step()
        return job

    def finished(arrays):
        shape = arrays[0].shape
        return launch(
            finish, [(shape, f32), ((8, shape[1]), f32)], arrays=arrays, pinned=False
        )

    s_att = None
    for level in reversed(range(LAYERS)):
        (
            (x_att, x_ffn, branch),
            (hidden, hidden_ffn, squares),
            (q_raw, k_raw, u_raw),
            (queries, keys, values, weights, incoming, mixed),
            (gate, up, product),
            (w_att, w_ffn),
        ) = stored[level]
        if back_ffn is None:
            back_ffn = head_gather(own)
            back_ffn[2] = tick(back_ffn[2], s_att, s_ffn)
        grad_gate, grad_up, *partial = launch(
            unit_back(rows),
            [unit_bf16] * 2 + block_out,
            (),
            (*back_ffn, gate, up, w_ffn),
        )
        first = head_scatter(partial)
        first[2] = tick(first[2], s_att)
        s_ffn = scatter(
            unit_weights, 3 * ffw, (grad_gate, grad_up, product, *hidden_ffn, *back_ffn)
        )
        grads, own, inner = launch(
            unit_norm_back,
            [row_out, ((rows, D), bf16), ((8, rows), f32)],
            arrays=(x_ffn, grads, branch, *first),
        )
        back_att = head_gather(own)
        back_att[2] = tick(back_att[2], s_att, s_ffn if level == 0 else None)
        inner = head_gather_small(inner)
        gated, grad_u, grad_mixed, states = launch(
            mixed_back(rows, level),
            [width_bf16, width_bf16, width_bf16, state_bf16],
            (info,),
            (*back_att, *squares, *inner, mixed, u_raw, queries, w_att, table),
        )
        other, moved = exchanged(
            states, info, table, level, count, False, lambda value: tick(value, s_ffn)
        )
        moved[-1] = tick(moved[-1], s_ffn)
        grad_q, key_part, value_part, hidden_part = launch(
            within_back(rows, level),
            [
                width_bf16,
                ((local_heads, capacity, 2 * HEAD_DIM), f32),
                width_f32,
                ((capacity, D), f32),
            ],
            (info,),
            (
                grad_mixed,
                grad_u,
                values,
                keys,
                queries,
                weights,
                incoming,
                q_raw,
                cosine,
                sine,
                w_att,
                table,
            ),
        )
        if level == 0:
            s_quo = scatter(
                lambda shapes: attention_weights(shapes, (0, 0, 1)),
                3 * att,
                (grad_q, grad_u, gated, *hidden, *back_att),
            )
        grad_k, grad_v, *partial = launch(
            keys_back(rows, level),
            [width_bf16, width_bf16] + block_out,
            (info,),
            (
                key_part,
                value_part,
                hidden_part,
                k_raw,
                keys,
                values,
                cosine,
                sine,
                w_att,
                table,
                states,
                other,
                *moved,
            ),
        )
        first = head_scatter(partial)
        first[2] = tick(first[2], s_ffn)
        if level == 0:
            s_kv = scatter(
                lambda shapes: attention_weights(shapes, (0, 0)),
                2 * att,
                (grad_k, grad_v, *hidden, *back_att),
            )
        else:
            s_att = scatter(
                lambda shapes: attention_weights(shapes, (0, 0, 0, 0, 1)),
                5 * att,
                (grad_k, grad_v, grad_q, grad_u, gated, *hidden, *back_att),
            )
        outputs = launch(
            attention_norm_back(count),
            [row_out] + [((rows, D), bf16)] * (level > 0),
            (info,),
            (x_att, grads, *first),
            pinned=level > 0,
        )
        grads, own = outputs[0], outputs[-1]
        back_ffn = None
        if level > 0:
            later_jobs = (s_att, s_ffn)
    grad_tokens = grads if aligned else from_ring(grads)

    total_att, squares_att = finished(later_jobs[0].parts_of_total())
    total_ffn, squares_ffn = finished(later_jobs[1].parts_of_total())
    first_ffn, squares_first = finished(s_ffn.parts_of_total())
    total_quo, squares_quo = finished(s_quo.parts_of_total())
    total_kv, squares_kv = finished(s_kv.parts_of_total())
    squares = squares_att + squares_ffn + squares_first + squares_quo + squares_kv
    for pairs in (NEAR, FAR):
        squares = squares + lax.ppermute(squares, "head", pairs)
    s = 1
    while s < count:
        squares = squares + lax.ppermute(squares, "dp", [(i, i ^ s) for i in range(count)])
        s *= 2
    first_att = jnp.concatenate([total_kv, total_quo], axis=0)
    kinds = [[(w.shape, f32)] * 3 for w in (w_qkvu, w_out, g_in, w_down)]
    (
        moment_qkvu,
        average_qkvu,
        weight_qkvu,
        moment_out,
        average_out,
        weight_out,
        grad_norm,
    ) = launch(
        renew_attention,
        kinds[0] + kinds[1] + [((8, 128), f32)],
        arrays=(squares, w_qkvu, m_qkvu, e_qkvu, w_out, m_out, e_out, first_att, total_att),
        pinned=False,
    )
    moment_gu, average_gu, weight_gu, moment_down, average_down, weight_down = launch(
        renew_unit,
        kinds[2] + kinds[3],
        arrays=(squares, g_in, m_in, e_in, w_down, m_down, e_down, first_ffn, total_ffn),
    )
    grad_norm = grad_norm[0, 0]
    moment_gu, average_gu, weight_gu = (
        jnp.swapaxes(a, 2, 3) for a in (moment_gu, average_gu, weight_gu)
    )
    return (
        out_tokens,
        grad_tokens,
        grad_norm,
        moment_qkvu,
        moment_out,
        moment_gu,
        moment_down,
        average_qkvu,
        average_out,
        average_gu,
        average_down,
        weight_qkvu,
        weight_out,
        weight_gu,
        weight_down,
    )


def solution(mesh):
    rows = P(("dp", "head"), None)
    by_row = P(None, None, "dp", "head")
    by_column = P(None, "head", "dp")
    weights = (by_row, by_column, by_row, by_column)
    return jax.shard_map(
        per_device,
        mesh=mesh,
        in_specs=(rows, P("dp", None), P()) + weights * 3,
        out_specs=(rows, rows, P()) + weights * 3,
        check_vma=False,
    )
```

```python
import math

import jax
import jax.numpy as jnp
from jax import lax
from jax.experimental import pallas as pl
from jax.experimental.pallas import tpu as pltpu
from jax.sharding import PartitionSpec as P

D = 1024
HEADS = 8
HEAD_DIM = 128
FF = 2816
DEPTH = 24
LAYERS = 2
FIRST_LAYER = 21

COST = 1.2
EXTRA = 16

epsilon = 1e-06
bf16 = jnp.bfloat16
f32 = jnp.float32


def dot_nn(a, b):
    return lax.dot_general(a, b, (((1,), (0,)), ((), ())), preferred_element_type=f32)


def dot_nt(a, b):
    return lax.dot_general(a, b, (((1,), (1,)), ((), ())), preferred_element_type=f32)


def dot_tn(a, b):
    return lax.dot_general(a, b, (((0,), (0,)), ((), ())), preferred_element_type=f32)


def ring_order(count):
    return list(range(0, count, 2)) + list(range(1, count, 2))[::-1]


def ring_pairs(count):
    order = ring_order(count)
    ahead = [(order[i], order[(i + 1) % count]) for i in range(count)]
    return ahead, [(b, a) for a, b in ahead]


def tie(value, *others):
    return lax.optimization_barrier((value,) + others)[0]


class Gather:
    def __init__(self, shard, count):
        self.pairs = ring_pairs(count)
        self.count = count
        self.hops = 0
        self.pieces = [shard] + [None] * (count - 1)
        self.moving = (shard, shard)

    def step(self):
        self.hops += 1
        k, count = self.hops, self.count
        ahead, behind = self.moving
        if k == count // 2:
            half = ahead.shape[0] // 2
            ahead, behind = ahead[:half], behind[half:]
        ahead = lax.ppermute(ahead, "dp", self.pairs[0])
        behind = lax.ppermute(behind, "dp", self.pairs[1])
        self.moving = (ahead, behind)
        if k == count // 2:
            self.pieces[k] = (ahead, behind)
        else:
            self.pieces[k], self.pieces[count - k] = ahead, behind

    def pass_through(self, value):
        value, *moving = lax.optimization_barrier((value, *self.moving))
        self.moving = tuple(moving)
        return value

    def after(self, *values):
        self.moving = lax.optimization_barrier((*self.moving, *values))[:2]

    def before(self, value):
        return tie(value, *self.moving)

    def weight(self):
        while self.hops < self.count // 2:
            self.step()
        pieces, half = self.pieces, self.count // 2
        if pieces[0].shape[1] % 128:
            pieces = [jnp.concatenate(p, axis=0) if k == half else p for k, p in enumerate(pieces)]
            return Weight([jnp.concatenate(pieces, axis=1)], [(0, 0)])
        arrays, places = [], []
        for k, piece in enumerate(pieces):
            column = k * pieces[0].shape[1]
            if k == half:
                arrays += list(piece)
                places += [(0, column), (piece[0].shape[0], column)]
            else:
                arrays.append(piece)
                places.append((0, column))
        return Weight(arrays, places)


def owner_of(group, k, count):
    here = jnp.where(group % 2 == 0, group // 2, count - 1 - group // 2)
    place = (here - k + count) % count
    return jnp.where(place < count // 2, 2 * place, 2 * (count - 1 - place) + 1)


class Weight:
    def __init__(self, arrays, places):
        self.arrays, self.places = arrays, places

    def arrivals(self):
        return pltpu.SemaphoreType.DMA((len(self.arrays),))

    def copies(self, refs, whole, arrived, low, high):
        out = []
        for i, (ref, (row, column)) in enumerate(zip(refs, self.places)):
            first, after = max(low, row), min(high, row + ref.shape[0])
            if first < after:
                out.append(
                    pltpu.make_async_copy(
                        ref.at[pl.ds(first - row, after - first), :],
                        whole.at[pl.ds(first, after - first), pl.ds(column, ref.shape[1])],
                        arrived.at[i],
                    )
                )
        return out


def piece_shapes(rows, count):
    part = D // count
    if part % 128:
        return [((rows, D), 0, 0)]
    out = []
    for k in range(count):
        if k == count // 2:
            out += [((rows // 2, part), 0, k * part), ((rows // 2, part), rows // 2, k * part)]
        else:
            out.append(((rows, part), 0, k * part))
    return out


def store_pieces(refs, shapes, value, low):
    for ref, (shape, row, column) in zip(refs, shapes):
        first, after = max(low, row), min(low + value.shape[0], row + shape[0])
        if first < after:
            ref[first - row : after - row, :] = value[
                first - low : after - low, column : column + shape[1]
            ].astype(ref.dtype)


def pieces_of(outputs, count):
    if len(outputs) == 1:
        whole, part, half = outputs[0], D // count, outputs[0].shape[0] // 2
        pieces = [whole[:, k * part : (k + 1) * part] for k in range(count)]
        middle = pieces[count // 2]
        pieces[count // 2] = (middle[:half], middle[half:])
        return pieces
    middle = count // 2
    return outputs[:middle] + [tuple(outputs[middle : middle + 2])] + outputs[middle + 2 :]


class Scatter:
    def __init__(self, pieces, count):
        self.pairs = ring_pairs(count)
        self.count = count
        self.hops = 0
        self.pieces = pieces
        self.moving = pieces[count // 2][::-1]
        self.closed = False

    def step(self):
        self.hops += 1
        k, count = self.count // 2 - self.hops, self.count
        ahead = lax.ppermute(self.moving[0], "dp", self.pairs[0])
        behind = lax.ppermute(self.moving[1], "dp", self.pairs[1])
        if k:
            mine = (self.pieces[count - k], self.pieces[k])
            self.moving = launch(
                add_on_the_way,
                [(piece.shape, bf16) for piece in mine],
                arrays=(*mine, ahead, behind),
            )
        else:
            self.moving = (ahead, behind)

    def pass_through(self, value):
        value, *moving = lax.optimization_barrier((value, *self.moving))
        self.moving = tuple(moving)
        return value

    def after(self, *values):
        self.moving = lax.optimization_barrier((*self.moving, *values))[:2]

    def before(self, value):
        return tie(value, *self.moving)

    def parts_of_total(self):
        while self.hops < self.count // 2:
            self.step()
        return [self.pieces[0], *self.moving]


def add_on_the_way(_, arrays, __, outs, ___):
    for i in range(2):
        mine, moving, out = arrays[i], arrays[2 + i], outs[i]
        rows, half = mine.shape[0], moving.shape[0]
        first = rows - half if i == 0 else 0
        if half < rows:
            rest = slice(0, half) if i == 0 else slice(half, rows)
            out[rest, :] = mine[rest, :]
        at = slice(first, first + half)
        out[at, :] = (mine[at, :].astype(f32) + moving[...].astype(f32)).astype(bf16)


def timed(us, body):
    body.us = us
    return body


def launch(body, outputs, scalars=(), arrays=(), parts=(), scratch=()):
    counts = [len(scalars), len(arrays), len(parts), len(outputs), len(scratch)]

    def kernel(*refs):
        groups, at = [], 0
        for size in counts:
            groups.append(refs[at : at + size])
            at += size
        body(*groups)

    spaces = (
        [pltpu.SMEM] * len(scalars) + [pltpu.VMEM] * len(arrays) + [pltpu.HBM] * len(parts)
    )
    return pl.pallas_call(
        kernel,
        out_shape=[
            (space[0] if space else jax.ShapeDtypeStruct)(shape, kind)
            for shape, kind, *space in outputs
        ],
        in_specs=[pl.BlockSpec(memory_space=space) for space in spaces],
        out_specs=[
            pl.BlockSpec(memory_space=pl.ANY if len(out) > 3 else pltpu.VMEM) for out in outputs
        ],
        scratch_shapes=list(scratch),
        compiler_params=pltpu.CompilerParams(vmem_limit_bytes=16 * 1024 * 1024),
        cost_estimate=pl.CostEstimate(
            flops=int(COST * 1e9 * getattr(body, "us", 1.0)), bytes_accessed=0, transcendentals=0
        ),
        name=body.__name__,
    )(*scalars, *arrays, *parts)


NEAR = [(0, 1), (1, 0), (2, 3), (3, 2)]
FAR = [(0, 2), (2, 0), (1, 3), (3, 1)]
CROSS = [(0, 3), (3, 0), (1, 2), (2, 1)]


def head_gather(block, tie_in=None):
    far = lax.ppermute(block, "head", FAR)
    if tie_in is not None:
        far = tie_in(far)
    near = lax.ppermute(block, "head", NEAR)
    cross = lax.ppermute(far, "head", NEAR)
    return [block, near, far, cross]


def add_blocks(_, arrays, __, outs, ___):
    a, b = arrays
    outs[0][...] = (a[...].astype(f32) + b[...].astype(f32)).astype(bf16)
    rows = a.shape[0] // 128 * 128
    if rows < a.shape[0]:
        pack(outs[0], unpack(a, 0, rows) + unpack(b, 0, rows))


def head_scatter(blocks, tie_in=None):
    near = lax.ppermute(blocks[1], "head", NEAR)
    cross = lax.ppermute(blocks[3], "head", NEAR)
    (to_far,) = launch(
        add_blocks, [(cross.shape, bf16, pltpu.VMEM)], arrays=(blocks[2], cross)
    )
    if tie_in is not None:
        to_far = tie_in(to_far)
    far = lax.ppermute(to_far, "head", FAR)
    return [blocks[0], near, far]


def row_scale_of(values):
    return lax.rsqrt(jnp.mean(values * values, axis=-1, keepdims=True) + epsilon)


def norm_back(values, grads):
    factor = row_scale_of(values)
    inner = jnp.mean(values * grads, axis=-1, keepdims=True)
    return factor * grads - values * (factor * factor * factor) * inner


def silu(v):
    return v * jax.nn.sigmoid(v)


def segment_of(places, seq_ends):
    return jnp.sum((places[..., None] >= seq_ends).astype(jnp.int32), axis=-1, dtype=jnp.int32)


def sequence_ends(info):
    ends, end = [], 0
    for i in range(2, info.shape[0]):
        end = end + info[i]
        ends.append(end)
    return ends


def group_layout(info, shape, dim, rows):
    index = lax.broadcasted_iota(jnp.int32, shape, dim)
    local = ((index // rows) ^ info[1]) * rows + index % rows
    place = local + info[0] * (4 * rows)
    segment = jnp.zeros(shape, jnp.int32)
    for end in sequence_ends(info):
        segment = segment + jnp.where(place >= end, 1, 0)
    return local.astype(f32), place, segment


def segment_at(info, place):
    segment = 0
    for end in sequence_ends(info):
        segment = segment + jnp.where(place >= end, 1, 0)
    return segment


def slope_of(table, level, h, local_heads):
    row = level * local_heads + h
    return table[row : row + 1, 127:128]


def query_decays(info, table, level, local_heads, rows):
    position, _, segment = group_layout(info, (4 * rows, 1), 0, rows)
    seqs = info.shape[0] - 2
    inward = (segment == segment_at(info, info[0] * (4 * rows) - 1)) & (segment < seqs)
    return [
        jnp.where(inward, jnp.exp(-slope_of(table, level, h, local_heads) * (position + 1.0)), 0.0)
        for h in range(local_heads)
    ]


def key_decays(info, table, level, local_heads, rows):
    position, _, segment = group_layout(info, (4 * rows, 1), 0, rows)
    seqs, size = info.shape[0] - 2, 4 * rows
    outward = (segment == segment_at(info, info[0] * size + (size - 1))) & (segment < seqs)
    return [
        jnp.where(
            outward,
            jnp.exp(-slope_of(table, level, h, local_heads) * (size - 1.0 - position)),
            0.0,
        )
        for h in range(local_heads)
    ]


def decay_parts(info, rows):
    size, seqs = 4 * rows, info.shape[0] - 2
    row_place, _, row_segment = group_layout(info, (size, 1), 0, rows)
    column_place, _, column_segment = group_layout(info, (1, size), 1, rows)
    apart = row_place - column_place
    allowed = (apart >= 0.0) & (row_segment == column_segment) & (row_segment < seqs)
    return jnp.maximum(apart, 0.0), allowed


def ring_columns(info, k, count, part):
    if part % 128:
        return slice(k * part, (k + 1) * part)
    return pl.ds(pl.multiple_of(owner_of(info[0], k, count) * part, 128), part)


def set_out(count, local_heads):
    def body(scalars, arrays, _, outs, __):
        info, tokens = scalars[0], arrays[0]
        x, hidden, cosine, sine, table = outs
        rows, part = tokens.shape[0], D // count
        for k in range(count):
            x[:, k * part : (k + 1) * part] = tokens[:, ring_columns(info, k, count, part)]
        values = x[...]
        hidden[...] = (values * row_scale_of(values)).astype(bf16)
        size = 4 * rows
        _, place, segment = group_layout(info, (size, 1), 0, rows)
        begins, end = jnp.zeros((size, 1), jnp.int32), 0
        for i in range(info.shape[0] - 2):
            begins = begins + jnp.where(segment == i, end, 0)
            end = end + info[2 + i]
        lane = lax.broadcasted_iota(jnp.int32, (1, HEAD_DIM), 1).astype(f32)
        frequency = jnp.exp(-math.log(10000.0) * lane / HEAD_DIM)
        angles = (place - begins).astype(f32) * frequency
        cosine[...] = jnp.cos(angles)
        sine[...] = jnp.sin(angles)
        row = lax.broadcasted_iota(jnp.int32, (8, 128), 0)
        lane = lax.broadcasted_iota(jnp.int32, (8, 128), 1)
        head = info[1] * local_heads + row % local_heads
        depth = (FIRST_LAYER + row // local_heads).astype(f32)
        base = jnp.exp(-8.0 * math.log(2.0) * (head + 1).astype(f32) / HEADS)
        slope = base * (1.0 - depth / (DEPTH - 1.0) + 1e-05)
        pairs = count // 2
        pair = info[0] // 2
        first = 2 * pair
        before = first * 0 + 2 * ((lane - 1) ^ pair)
        after = 2 * ((lane - pairs) ^ pair)
        low = jnp.where(lane < 2, first + lane, jnp.where(lane <= pairs, before + 2, first + 2))
        high = jnp.where(lane < 2, first + lane + 1, jnp.where(lane <= pairs, first, after))
        broken = jnp.where(high < low, 1, 0)
        for g in range(count):
            begin, last = segment_at(info, g * size), segment_at(info, (g + 1) * size - 1)
            joined = jnp.where(begin == last, 1, 0) * jnp.where(last < info.shape[0] - 2, 1, 0)
            broken = broken + jnp.where((low <= g) & (g < high), 1 - joined, 0)
        steps = jnp.maximum(high - low, 0).astype(f32)
        factors = jnp.where(broken == 0, jnp.exp(-slope * size * steps), 0.0)
        table[...] = jnp.where(lane == 127, slope, factors)

    return body


def take_cotangent(count):
    def body(scalars, arrays, _, outs, __):
        info, cotangent = scalars[0], arrays[0]
        rows, part = cotangent.shape[0] // 4, D // count
        _, _, segment = group_layout(info, (4 * rows, 1), 0, rows)
        live = jnp.where(segment < info.shape[0] - 2, 1.0, 0.0)
        for j in range(4):
            at = pl.ds(pl.multiple_of((info[1] ^ j) * rows, rows), rows)
            for k in range(count):
                columns = slice(k * part, (k + 1) * part)
                value = cotangent[at, ring_columns(info, k, count, part)]
                value = value * live[j * rows : (j + 1) * rows, :]
                if j == 0:
                    outs[0][:, columns] = value
                outs[1 + j][:, columns] = value.astype(bf16)

    return body


def store_natural(ref, info, value, count):
    part = D // count
    for k in range(count):
        ref[:, ring_columns(info, k, count, part)] = value[:, k * part : (k + 1) * part]


def stacked(refs, rows=None):
    return jnp.concatenate([ref[:rows, :] for ref in refs], axis=0)


def pack(ref, *values):
    start, size = ref.shape[0] - EXTRA, values[0].shape[1]
    row = lax.broadcasted_iota(jnp.int32, (EXTRA, size), 0)
    out = jnp.zeros((EXTRA, size), f32)
    for i, value in enumerate(values):
        high = value.astype(bf16).astype(f32)
        out = jnp.where(row == 2 * i, high, out)
        out = jnp.where(row == 2 * i + 1, value - high, out)
    if size < ref.shape[1]:
        ref[start:, size:] = jnp.zeros((EXTRA, ref.shape[1] - size), bf16)
    ref[start:, :size] = out.astype(bf16)


def unpack(ref, i, size):
    rest = ref[ref.shape[0] - EXTRA :, :size].astype(f32)
    return rest[2 * i : 2 * i + 1, :] + rest[2 * i + 1 : 2 * i + 2, :]


def rotated(active, cosine, sine):
    return jnp.concatenate([active * cosine, active * sine], axis=1).astype(bf16)


def head_columns(h):
    return slice(h * HEAD_DIM, (h + 1) * HEAD_DIM)


def row_of_sums(values):
    ones = jnp.ones((8, values.shape[1]), f32)
    return lax.dot_general(
        ones, values, (((1,), (1,)), ((), ())), precision=lax.Precision.HIGHEST,
        preferred_element_type=f32,
    )


def column_of(row):
    size = row.shape[1]
    same = lax.broadcasted_iota(jnp.int32, (size, size), 0) == lax.broadcasted_iota(
        jnp.int32, (size, size), 1
    )
    return jnp.sum(jnp.where(same, jnp.broadcast_to(row, (size, size)), 0.0), axis=1, keepdims=True)


def prepare_attention(level):
    def prepare(_, arrays, __, outs, ___):
        w_qkvu, w_out = arrays
        size = w_out.shape[1]
        for i, which in enumerate((1, 2, 0, 3)):
            outs[0][i * size : (i + 1) * size, :] = jnp.transpose(w_qkvu[level, which]).astype(bf16)
        outs[0][4 * size :, :] = w_out[level].astype(bf16)

    return prepare


def prepare_unit(level):
    def prepare(_, arrays, __, outs, ___):
        w_gu, w_down = arrays
        size = w_down.shape[1]
        for i in range(2):
            outs[0][i * size : (i + 1) * size, :] = w_gu[level, i].astype(bf16)
        outs[0][2 * size :, :] = w_down[level].astype(bf16)

    return prepare


def block_copies(refs, whole, arrived):
    rows = refs[0].shape[0]
    return [
        pltpu.make_async_copy(ref, whole.at[pl.ds(j * rows, rows), :], arrived.at[j])
        for j, ref in enumerate(refs)
    ]


def keys_values(weight, rows, level):
    def body(scalars, arrays, parts, outs, scratch):
        (info,) = scalars
        cosine, sine, table = arrays[4:]
        k_raw, keys, values, states, whole, kept_keys, kept_values, kept_hidden, kept_whole = outs
        heads = states.shape[0]
        att = k_raw.shape[1]
        copies = weight.copies(parts, whole, scratch[0], 0, 2 * att)
        later = weight.copies(parts, whole, scratch[1], 2 * att, 5 * att)
        later += weight.copies(parts, kept_whole, scratch[2], 0, 5 * att)
        later += block_copies(arrays[:4], kept_hidden, scratch[3])
        for copy in copies + later:
            copy.start()
        decays = key_decays(info, table, level, heads, rows)
        hidden = stacked(arrays[:4])
        for copy in copies:
            copy.wait()
        for h in range(heads):
            cols = head_columns(h)
            raw = dot_nt(hidden, whole[h * HEAD_DIM : (h + 1) * HEAD_DIM, :])
            k_raw[:, cols] = raw
            key = rotated(silu(raw), cosine[...], sine[...])
            keys[h] = key
            kept_keys[h] = key
            at = att + h * HEAD_DIM
            value = dot_nt(hidden, whole[at : at + HEAD_DIM, :]).astype(bf16)
            values[:, cols] = value
            kept_values[:, cols] = value
            decayed = (key.astype(f32) * decays[h]).astype(bf16)
            states[h] = dot_tn(decayed, value).astype(bf16)
        for copy in later:
            copy.wait()

    return body


def pair_states(forward, level):
    def body(scalars, arrays, _, outs, __):
        (info,) = scalars
        table, own, other = arrays
        heads = own.shape[0]
        even = jnp.where(info[0] % 2 == 0, 1.0, 0.0)
        for h in range(heads):
            row = level * heads + h
            a, b = own[h].astype(f32), other[h].astype(f32)
            low, high = even * a + (1.0 - even) * b, even * b + (1.0 - even) * a
            if forward:
                both = table[row : row + 1, 1:2] * low + high
            else:
                both = low + table[row : row + 1, 0:1] * high
            outs[0][h] = both.astype(bf16)

    return body


def carried_state(info, table, level, own, other, moved, h, forward):
    row, pairs = level * own.shape[0] + h, len(moved)
    even = jnp.where(info[0] % 2 == 0, 1.0, 0.0)
    total = jnp.zeros(own.shape[1:], f32)
    for i, ref in enumerate(moved):
        at = 2 + i + (0 if forward else pairs)
        total = total + table[row : row + 1, at : at + 1] * ref[h].astype(f32)
    if forward:
        step = table[row : row + 1, 0:1] * total + other[h].astype(f32)
        total = even * total + (1.0 - even) * step
    else:
        step = table[row : row + 1, 1:2] * total + other[h].astype(f32)
        total = even * step + (1.0 - even) * total
    return total.astype(bf16)


def within_group(rows, level):
    def body(scalars, arrays, parts, outs, scratch):
        (info,) = scalars
        cosine, sine, keys, values, whole, table = arrays[4:]
        q_raw, u_raw, queries, weights, within, kept_u, kept_queries = outs
        heads = weights.shape[0]
        att = q_raw.shape[1]
        apart, allowed = decay_parts(info, rows)
        hidden = stacked(arrays[:4])
        for h in range(heads):
            cols = head_columns(h)
            at = 2 * att + h * HEAD_DIM
            raw = dot_nt(hidden, whole[at : at + HEAD_DIM, :])
            q_raw[:, cols] = raw
            query = rotated(silu(raw), cosine[...], sine[...])
            queries[h] = query
            kept_queries[h] = query
            decay = jnp.where(allowed, jnp.exp(-slope_of(table, level, h, heads) * apart), 0.0)
            score = (dot_nt(query, keys[h]) * decay).astype(bf16)
            weights[h] = score
            within[:, cols] = dot_nn(score, values[:, cols])
        u = dot_nt(hidden, whole[3 * att : 4 * att, :])
        u_raw[...] = u
        kept_u[...] = u

    return body


def mix(rows, level):
    def body(scalars, arrays, parts, outs, scratch):
        (info,) = scalars
        whole, table, queries, within, u_raw, own, other = arrays[:7]
        moved = arrays[7:]
        mixed, incoming = outs[:2]
        att, heads = mixed.shape[1], own.shape[0]
        decays = query_decays(info, table, level, heads, rows)
        gated = []
        for h in range(heads):
            cols = head_columns(h)
            state = carried_state(info, table, level, own, other, moved, h, True)
            incoming[h] = state
            value = within[:, cols] + decays[h] * dot_nn(queries[h], state)
            mixed[:, cols] = value
            gated.append((value * u_raw[:, cols]).astype(bf16))
        gated = jnp.concatenate(gated, axis=1)
        squares = row_of_sums(mixed[...] * mixed[...])
        for j, ref in enumerate(outs[2:]):
            block = slice(j * rows, (j + 1) * rows)
            ref[:rows, :] = dot_nn(gated[block, :], whole[4 * att :, :]).astype(bf16)
            pack(ref, squares[0:1, block])

    return body


def add_attention(_, arrays, __, outs, ___):
    x, *blocks = arrays
    x_out, branch, hidden, squares, kept_x, kept_out = outs
    rows = x.shape[0]
    total, squared = 0.0, 0.0
    for ref in blocks:
        total = total + ref[:rows, :].astype(f32)
        squared = squared + unpack(ref, 0, rows)
    squares[...] = jnp.broadcast_to(squared, squares.shape)
    branch[...] = total
    value = x[...] + total * lax.rsqrt(column_of(squared) / D + epsilon)
    x_out[...] = value
    kept_out[...] = value
    kept_x[...] = x[...]
    hidden[...] = (value * row_scale_of(value)).astype(bf16)


def add_unit(count):
    def body(scalars, arrays, __, outs, ___):
        x, first, near, far = arrays
        value = x[...] + (first[...].astype(f32) + near[...].astype(f32) + far[...].astype(f32))
        if len(outs) > 1:
            outs[0][...] = value
            outs[1][...] = (value * row_scale_of(value)).astype(bf16)
        else:
            store_natural(outs[0], scalars[0], value, count)

    return body


def gated_unit(weight, rows, last):
    def body(_, arrays, parts, outs, scratch):
        gate, up, product, kept_hidden, kept_whole = outs[:5]
        whole = kept_whole if last else scratch[0]
        ffw = gate.shape[1]
        copies = [
            weight.copies(parts, whole, scratch[1 + i], i * ffw, (i + 1) * ffw) for i in range(3)
        ]
        later = block_copies(arrays, kept_hidden, scratch[5])
        if not last:
            later += weight.copies(parts, kept_whole, scratch[4], 0, 3 * ffw)
        for copy in sum(copies, []) + later:
            copy.start()
        hidden = stacked(arrays)
        for copy in copies[0]:
            copy.wait()
        a = dot_nt(hidden, whole[:ffw, :])
        for copy in copies[1]:
            copy.wait()
        b = dot_nt(hidden, whole[ffw : 2 * ffw, :])
        gate[...] = a.astype(bf16)
        up[...] = b.astype(bf16)
        value = (a * b).astype(bf16)
        product[...] = value
        for copy in copies[2]:
            copy.wait()
        for j, ref in enumerate(outs[5:]):
            ref[...] = dot_nn(value[j * rows : (j + 1) * rows, :], whole[2 * ffw :, :]).astype(bf16)
        for copy in later:
            copy.wait()

    return body


def unit_back(rows):
    def body(_, arrays, parts, outs, scratch):
        gate, up, whole = arrays[4:]
        grad_gate, grad_up = outs[:2]
        ffw = gate.shape[1]
        back = stacked(arrays[:4])
        grad = dot_nt(back, whole[2 * ffw :, :])
        a = (grad * up[...].astype(f32)).astype(bf16)
        b = (grad * gate[...].astype(f32)).astype(bf16)
        grad_gate[...] = a
        grad_up[...] = b
        for j, ref in enumerate(outs[2:]):
            block = slice(j * rows, (j + 1) * rows)
            ref[...] = (
                dot_nn(a[block, :], whole[:ffw, :]) + dot_nn(b[block, :], whole[ffw : 2 * ffw, :])
            ).astype(bf16)

    return body


def unit_weights(shapes):
    def body(_, arrays, __, outs, ___):
        hidden, back = arrays[3][...], stacked(arrays[4:])
        ffw = arrays[0].shape[1]
        for i, right in enumerate((hidden, hidden, back)):
            store_pieces(outs, shapes, dot_tn(arrays[i][...], right), i * ffw)

    return body


def attention_weights(shapes, lefts):
    def body(_, arrays, __, outs, ___):
        hidden = arrays[-5][...]
        rights = [hidden, stacked(arrays[-4:], hidden.shape[0] // 4)]
        at = 0
        for i, which in enumerate(lefts):
            grad = dot_tn(arrays[i][...], rights[which])
            store_pieces(outs, shapes, grad, at)
            at += grad.shape[0]

    return body


def back_through_norm(x, grads, arrays):
    first, near, far = arrays
    incoming = first[...].astype(f32) + near[...].astype(f32) + far[...].astype(f32)
    return grads[...] + norm_back(x[...], incoming)


def unit_norm_back(_, arrays, __, outs, ___):
    x, grads, branch, squares = arrays[:4]
    new, own = outs
    value = back_through_norm(x, grads, arrays[4:])
    new[...] = value
    rounded = value.astype(bf16)
    own[: x.shape[0], :] = rounded
    inner = row_of_sums(rounded.astype(f32) * branch[...])
    pack(own, inner[0:1, :], squares[0:1, :])


def attention_norm_back(count):
    def body(scalars, arrays, __, outs, ___):
        x, grads = arrays[:2]
        value = back_through_norm(x, grads, arrays[2:])
        if len(outs) > 1:
            outs[0][...] = value
            outs[1][...] = value.astype(bf16)
        else:
            store_natural(outs[0], scalars[0], value, count)

    return body


def mixed_back(rows, level):
    def body(scalars, arrays, parts, outs, scratch):
        (info,) = scalars
        back_refs = arrays[:4]
        mixed, u_raw, queries, whole, table = arrays[4:]
        gated, grad_u, grad_mixed, states = outs
        att, heads = mixed.shape[1], states.shape[0]
        decays = query_decays(info, table, level, heads, rows)
        inner, squares = (
            jnp.concatenate([column_of(unpack(ref, i, rows)) for ref in back_refs], axis=0)
            for i in range(2)
        )
        scale = lax.rsqrt(squares / D + epsilon)
        factor = scale * scale * inner / D
        back = stacked(back_refs, rows)
        grad_gated = dot_nt(back, whole[4 * att :, :])
        value, u = mixed[...], u_raw[...]
        normed = value * scale
        gated[...] = (normed * u).astype(bf16)
        grad_u[...] = (grad_gated * normed).astype(bf16)
        grad = (scale * (grad_gated * u) - value * (scale * factor)).astype(bf16)
        grad_mixed[...] = grad
        for h in range(heads):
            weighted = (queries[h].astype(f32) * decays[h]).astype(bf16)
            states[h] = dot_tn(weighted, grad[:, head_columns(h)]).astype(bf16)

    return body


def unrotated(grad, raw, cosine, sine):
    active = grad[:, :HEAD_DIM] * cosine + grad[:, HEAD_DIM:] * sine
    sigma = jax.nn.sigmoid(raw)
    return active * (sigma * (1.0 + raw * (1.0 - sigma)))


def within_back(rows, level):
    def body(scalars, arrays, parts, outs, scratch):
        (info,) = scalars
        grad_mixed, grad_u, values, keys, queries, weights, incoming, q_raw = arrays[:8]
        cosine, sine, whole, table = arrays[8:]
        grad_q, key_part, value_part, hidden_part = outs
        att, heads = q_raw.shape[1], weights.shape[0]
        apart, allowed = decay_parts(info, rows)
        decays = query_decays(info, table, level, heads, rows)
        for h in range(heads):
            cols = head_columns(h)
            grad = grad_mixed[:, cols]
            decay = jnp.where(allowed, jnp.exp(-slope_of(table, level, h, heads) * apart), 0.0)
            scores = (dot_nt(grad, values[:, cols]) * decay).astype(bf16)
            to_query = dot_nn(scores, keys[h]) + decays[h] * dot_nt(grad, incoming[h])
            grad_q[:, cols] = unrotated(
                to_query, q_raw[:, cols], cosine[...], sine[...]
            ).astype(bf16)
            key_part[h] = dot_tn(scores, queries[h])
            value_part[:, cols] = dot_tn(weights[h], grad)
        hidden_part[...] = dot_nn(grad_q[...], whole[2 * att : 3 * att, :]) + dot_nn(
            grad_u[...], whole[3 * att : 4 * att, :]
        )

    return body


def keys_back(rows, level):
    def body(scalars, arrays, parts, outs, scratch):
        (info,) = scalars
        key_part, value_part, hidden_part, k_raw, keys, values, cosine, sine = arrays[:8]
        whole, table, own, other = arrays[8:12]
        moved = arrays[12:]
        grad_k, grad_v = outs[:2]
        att, heads = k_raw.shape[1], own.shape[0]
        decays = key_decays(info, table, level, heads, rows)
        for h in range(heads):
            cols = head_columns(h)
            state = carried_state(info, table, level, own, other, moved, h, False)
            key, value = keys[h], values[:, cols]
            to_key = key_part[h] + decays[h] * dot_nt(value, state)
            decayed = (key.astype(f32) * decays[h]).astype(bf16)
            grad_v[:, cols] = (value_part[:, cols] + dot_nn(decayed, state)).astype(bf16)
            grad_k[:, cols] = unrotated(
                to_key, k_raw[:, cols], cosine[...], sine[...]
            ).astype(bf16)
        for j, ref in enumerate(outs[2:]):
            block = slice(j * rows, (j + 1) * rows)
            ref[...] = (
                hidden_part[block, :]
                + dot_nn(grad_k[block, :], whole[:att, :])
                + dot_nn(grad_v[block, :], whole[att : 2 * att, :])
            ).astype(bf16)

    return body


def finish(_, arrays, __, outs, ___):
    total = arrays[0][...].astype(f32)
    for ref in arrays[1:]:
        total = total + ref[...].astype(f32)
    outs[0][...] = total
    squares = total * total
    outs[1][...] = jnp.sum(squares.reshape(-1, 8, squares.shape[1]), axis=0)


def step_sizes(squares):
    norm = jnp.sqrt(jnp.full((8, 128), jnp.sum(squares[...]), f32))
    return norm, jnp.minimum(1.0, 1.0 / (norm + 1e-06))[0:1, 0:1]


def renew(refs, outs, at, gradient, factor):
    weight, moment, average = (ref[at] for ref in refs)
    rate = 0.1 * math.sqrt(LAYERS * (5 * D * D + 3 * D * FF) / D)
    clipped = gradient * factor
    new_moment = 0.9 * moment + clipped
    new_weight = weight - rate * (clipped + 0.9 * new_moment)
    outs[0][at] = new_moment
    outs[1][at] = 0.8 * average + 0.2 * new_weight
    outs[2][at] = new_weight


def renew_attention(_, arrays, __, outs, ___):
    norm, factor = step_sizes(arrays[0])
    size = arrays[4].shape[1]
    for level in range(LAYERS):
        total = arrays[7 + level]
        for i, which in enumerate((1, 2, 0, 3)):
            gradient = jnp.transpose(total[i * size : (i + 1) * size, :])
            renew(arrays[1:4], outs[:3], (level, which), gradient, factor)
        renew(arrays[4:7], outs[3:6], (level,), total[4 * size :, :], factor)
    outs[6][...] = norm


def renew_unit(_, arrays, __, outs, ___):
    _, factor = step_sizes(arrays[0])
    size = arrays[4].shape[1]
    for level in range(LAYERS):
        total = arrays[7 + level]
        for i in range(2):
            gradient = total[i * size : (i + 1) * size, :]
            renew(arrays[1:4], outs[:3], (level, i), gradient, factor)
        renew(arrays[4:7], outs[3:6], (level,), total[2 * size :, :], factor)


def exchanged(states, info, table, level, count, forward, hop):
    other = lax.ppermute(states, "dp", [(i, i ^ 1) for i in range(count)])
    other = hop(other)
    (both,) = launch(
        pair_states(forward, level), [(states.shape, bf16, pltpu.VMEM)], (info,), (table, states, other)
    )
    return other, [
        lax.ppermute(both, "dp", [(i, i ^ (2 * s)) for i in range(count)])
        for s in range(1, count // 2)
    ]


def per_device(
    tokens,
    cotangent,
    lengths,
    w_qkvu,
    w_out,
    w_gu,
    w_down,
    m_qkvu,
    m_out,
    m_gu,
    m_down,
    e_qkvu,
    e_out,
    e_gu,
    e_down,
):
    rows = tokens.shape[0]
    count = lax.axis_size("dp")
    ranks = lax.axis_size("head")
    group = lax.axis_index("dp")
    rank = lax.axis_index("head")
    capacity = rows * ranks
    local_heads = HEADS // ranks
    att = local_heads * HEAD_DIM
    ffw = FF // ranks
    part = D // count

    order = ring_order(count)
    place = [order.index(i) for i in range(count)]
    my_place = jnp.array(place, jnp.int32)[group]
    owners = [jnp.array(order, jnp.int32)[(my_place - k) % count] for k in range(count)]
    sources = [(my_place - place[c]) % count for c in range(count)]

    def to_ring(array):
        return jnp.concatenate(
            [lax.dynamic_slice_in_dim(array, owners[k] * part, part, 1) for k in range(count)], axis=1
        )

    def from_ring(array):
        return jnp.concatenate(
            [lax.dynamic_slice_in_dim(array, sources[c] * part, part, 1) for c in range(count)], axis=1
        )

    def here(*shape):
        return shape, f32, pltpu.VMEM

    def here_bf16(*shape):
        return shape, bf16, pltpu.VMEM

    def kept(*shape):
        return shape, f32, pltpu.HBM

    def kept_bf16(*shape):
        return shape, bf16, pltpu.HBM

    block_out = [here_bf16(rows, D)] * ranks
    row_out = here(rows, D)
    pair = (local_heads, capacity, 2 * HEAD_DIM)
    state = (local_heads, 2 * HEAD_DIM, HEAD_DIM)

    hops = count // 2
    aligned = part % 128 == 0
    g_in, m_in, e_in = (jnp.swapaxes(a, 2, 3) for a in (w_gu, m_gu, e_gu))
    (shard,) = launch(
        prepare_attention(0), [((5 * att, part), bf16)], arrays=(w_qkvu, w_out)
    )
    g_first = Gather(shard, count)
    g_first.step()
    info = jnp.concatenate([jnp.stack([group, rank]).astype(jnp.int32), lengths])
    x_att, own, cosine, sine, table = launch(
        set_out(count, local_heads),
        [
            row_out,
            here_bf16(rows, D),
            here(capacity, HEAD_DIM),
            here(capacity, HEAD_DIM),
            here(8, 128),
        ],
        (info,),
        (tokens if aligned else to_ring(tokens),),
    )
    g_first.after(own)
    g_first.step()
    hidden = head_gather(own)
    g_first.after(*hidden)
    while g_first.hops < hops:
        g_first.step()
    def prepared(level):
        (attention,) = launch(
            prepare_attention(level), [((5 * att, part), bf16)], arrays=(w_qkvu, w_out)
        )
        (unit,) = launch(prepare_unit(level), [((3 * ffw, part), bf16)], arrays=(g_in, w_down))
        return Gather(attention, count), Gather(unit, count)

    (unit,) = launch(prepare_unit(0), [((3 * ffw, part), bf16)], arrays=(g_in, w_down))
    ring = [Gather(unit, count)]
    for level in range(1, LAYERS):
        ring += prepared(level)

    def hop(value):
        for job in ring:
            if job.hops < hops:
                value = job.pass_through(value)
                job.step()
                break
        return value

    w_parts = g_first.weight()
    stored = []
    for level in range(LAYERS):
        last = level + 1 == LAYERS
        if level == 0:
            ring[0].after(*g_first.moving)
            ring[0].step()
        else:
            hidden = head_gather(hop(own), hop)
            w_parts = ring[2 * level - 1].weight()
            ring[2 * level].after(*ring[2 * level - 1].moving)
            ring[2 * level].step()
        k_raw, keys, values, states, w_att, *kept_att = launch(
            timed(5, keys_values(w_parts, rows, level)),
            [
                kept(capacity, att),
                here_bf16(*pair),
                here_bf16(capacity, att),
                here_bf16(*state),
                here_bf16(5 * att, D),
                kept_bf16(*pair),
                kept_bf16(capacity, att),
                (*kept_bf16(capacity, D), True),
                (*kept_bf16(5 * att, D), True),
            ],
            (info,),
            (*hidden, cosine, sine, table),
            w_parts.arrays,
            [w_parts.arrivals()] * 3 + [pltpu.SemaphoreType.DMA((ranks,))],
        )
        other, moved = exchanged(states, info, table, level, count, True, hop)
        q_raw, u_raw, queries, weights, within, kept_u, kept_queries = launch(
            timed(3.5, within_group(rows, level)),
            [
                kept(capacity, att),
                here(capacity, att),
                here_bf16(*pair),
                kept_bf16(local_heads, capacity, capacity),
                here(capacity, att),
                kept(capacity, att),
                kept_bf16(*pair),
            ],
            (info,),
            (*hidden, cosine, sine, keys, values, w_att, table),
        )
        mixed, incoming, *partial = launch(
            timed(2.5, mix(rows, level)),
            [kept(capacity, att), kept_bf16(*state)] + [here_bf16(rows + EXTRA, D)] * ranks,
            (info,),
            (w_att, table, queries, within, u_raw, states, other, *moved),
        )
        partial[3] = hop(partial[3])
        first = head_scatter(partial)
        x_ffn, branch, own, squares, kept_x_att, kept_x_ffn = launch(
            add_attention,
            [
                row_out,
                kept(rows, D),
                here_bf16(rows, D),
                here(8, rows),
                kept(rows, D),
                kept(rows, D),
            ],
            arrays=(x_att, *first),
        )
        hidden_ffn = head_gather(hop(own), lambda far: hop(ring[2 * level].pass_through(far)))
        w_parts = ring[2 * level].weight()
        gate, up, product, kept_hidden_ffn, w_ffn, *partial = launch(
            timed(7, gated_unit(w_parts, rows, last)),
            [(here_bf16 if last else kept_bf16)(capacity, ffw)] * 3
            + [(*kept_bf16(capacity, D), True)]
            + [here_bf16(3 * ffw, D) if last else (*kept_bf16(3 * ffw, D), True)]
            + block_out,
            (),
            hidden_ffn,
            w_parts.arrays,
            [pltpu.VMEM((16 if last else 3 * ffw, D), bf16)]
            + [w_parts.arrivals()] * 4
            + [pltpu.SemaphoreType.DMA((ranks,))],
        )
        partial[3] = hop(partial[3])
        first = head_scatter(partial)
        outputs = launch(
            add_unit(count),
            [kept(rows, D)] if last else [row_out, here_bf16(rows, D)],
            (info,),
            (x_ffn, *first),
        )
        kept_keys, kept_values, kept_hidden, kept_w_att = kept_att
        stored.append(
            (
                (kept_x_att, kept_x_ffn, branch),
                (kept_hidden, kept_hidden_ffn, squares),
                (q_raw, k_raw, kept_u),
                (kept_queries, kept_keys, kept_values, weights, incoming, mixed),
                (gate, up, product),
                (kept_w_att, w_ffn),
            )
        )
        x_att, own = outputs[0], outputs[-1]
    out_tokens = x_att if aligned else from_ring(x_att)

    grads, *back_ffn = launch(
        take_cotangent(count),
        [row_out] + block_out,
        (info,),
        (cotangent if aligned else to_ring(cotangent),),
    )

    def tick(value, *jobs):
        for job in jobs:
            if not job.closed:
                value = job.pass_through(value)
        for job in jobs:
            if not job.closed:
                value = job.pass_through(value)
                if job.hops < hops:
                    job.step()
                else:
                    job.closed = True
        return value

    def scatter(body, rows_out, arrays):
        shapes = piece_shapes(rows_out, count)
        outputs = launch(
            timed(rows_out / 800, body(shapes)),
            [(shape, bf16) for shape, _, _ in shapes],
            arrays=arrays,
        )
        job = Scatter(pieces_of(list(outputs), count), count)
        job.step()
        return job

    def finished(arrays):
        shape = arrays[0].shape
        return launch(
            finish, [(shape, f32), ((8, shape[1]), f32)], arrays=arrays
        )

    s_att = None
    for level in reversed(range(LAYERS)):
        (
            (x_att, x_ffn, branch),
            (hidden, hidden_ffn, squares),
            (q_raw, k_raw, u_raw),
            (queries, keys, values, weights, incoming, mixed),
            (gate, up, product),
            (w_att, w_ffn),
        ) = stored[level]
        if back_ffn is None:
            back_ffn = head_gather(tick(own, s_ffn, s_att))
        grad_gate, grad_up, *partial = launch(
            timed(3, unit_back(rows)),
            [here_bf16(capacity, ffw)] * 2 + block_out,
            (),
            (*back_ffn, gate, up, w_ffn),
        )
        if level == 0:
            partial[3] = tick(partial[3], s_att)
        first = head_scatter(partial)
        s_ffn = scatter(
            unit_weights, 3 * ffw, (grad_gate, grad_up, product, hidden_ffn, *back_ffn)
        )
        first[2] = tie(first[2], *s_ffn.pieces[0:1])
        grads, own = launch(
            unit_norm_back,
            [row_out, here_bf16(rows + EXTRA, D)],
            arrays=(x_ffn, grads, branch, squares, *first),
        )
        own = tick(own, *([s_att, s_ffn] if level == 0 else [s_ffn]))
        back_att = head_gather(own)
        gated, grad_u, grad_mixed, states = launch(
            timed(2, mixed_back(rows, level)),
            [here_bf16(capacity, att)] * 3 + [here_bf16(*state)],
            (info,),
            (*back_att, mixed, u_raw, queries, w_att, table),
        )
        other, moved = exchanged(
            states,
            info,
            table,
            level,
            count,
            False,
            lambda value: tick(value, *([s_att, s_ffn] if level == 0 else [s_ffn])),
        )
        grad_q, key_part, value_part, hidden_part = launch(
            timed(3.3, within_back(rows, level)),
            [here_bf16(capacity, att), here(*pair), here(capacity, att), here(capacity, D)],
            (info,),
            (
                grad_mixed,
                grad_u,
                values,
                keys,
                queries,
                weights,
                incoming,
                q_raw,
                cosine,
                sine,
                w_att,
                table,
            ),
        )
        if level > 0:
            moved[-1] = tick(moved[-1], s_ffn)
        else:
            s_quo = scatter(
                lambda shapes: attention_weights(shapes, (0, 0, 1)),
                3 * att,
                (grad_q, grad_u, gated, hidden, *back_att),
            )
            moved[-1] = tick(moved[-1], s_ffn, s_quo)
        grad_k, grad_v, *partial = launch(
            timed(2.1, keys_back(rows, level)),
            [here_bf16(capacity, att)] * 2 + block_out,
            (info,),
            (
                key_part,
                value_part,
                hidden_part,
                k_raw,
                keys,
                values,
                cosine,
                sine,
                w_att,
                table,
                states,
                other,
                *moved,
            ),
        )
        first = head_scatter(partial)
        if level == 0:
            s_kv = scatter(
                lambda shapes: attention_weights(shapes, (0, 0)),
                2 * att,
                (grad_k, grad_v, hidden, *back_att),
            )
        else:
            s_att = scatter(
                lambda shapes: attention_weights(shapes, (0, 0, 0, 0, 1)),
                5 * att,
                (grad_k, grad_v, grad_q, grad_u, gated, hidden, *back_att),
            )
        if level > 0:
            first[2] = tie(first[2], s_att.pieces[0])
        else:
            first[2] = tick(first[2], s_kv, s_quo, s_ffn)
        outputs = launch(
            attention_norm_back(count),
            [row_out, here_bf16(rows, D)] if level > 0 else [kept(rows, D)],
            (info,),
            (x_att, grads, *first),
        )
        grads, own = outputs[0], outputs[-1]
        if level == 0:
            grads = tick(grads, s_kv, s_quo)
        back_ffn = None
        if level > 0:
            later_jobs = (s_att, s_ffn)
    grad_tokens = grads if aligned else from_ring(grads)

    total_att, squares_att = finished(later_jobs[0].parts_of_total())
    total_ffn, squares_ffn = finished(later_jobs[1].parts_of_total())
    first_ffn, squares_first = finished(s_ffn.parts_of_total())
    total_quo, squares_quo = finished(s_quo.parts_of_total())
    total_kv, squares_kv = finished(s_kv.parts_of_total())
    squares = squares_att + squares_ffn + squares_first + squares_quo + squares_kv
    for pairs in (NEAR, FAR):
        squares = squares + lax.ppermute(squares, "head", pairs)
    s = 1
    while s < count:
        squares = squares + lax.ppermute(squares, "dp", [(i, i ^ s) for i in range(count)])
        s *= 2
    first_att = jnp.concatenate([total_kv, total_quo], axis=0)
    kinds = [[kept(*w.shape)] * 3 for w in (w_qkvu, w_out, g_in, w_down)]
    (
        moment_qkvu,
        average_qkvu,
        weight_qkvu,
        moment_out,
        average_out,
        weight_out,
        grad_norm,
    ) = launch(
        timed(3, renew_attention),
        kinds[0] + kinds[1] + [((8, 128), f32)],
        arrays=(squares, w_qkvu, m_qkvu, e_qkvu, w_out, m_out, e_out, first_att, total_att),
    )
    moment_gu, average_gu, weight_gu, moment_down, average_down, weight_down = launch(
        timed(4, renew_unit),
        kinds[2] + kinds[3],
        arrays=(squares, g_in, m_in, e_in, w_down, m_down, e_down, first_ffn, total_ffn),
    )
    grad_norm = grad_norm[0, 0]
    moment_gu, average_gu, weight_gu = (
        jnp.swapaxes(a, 2, 3) for a in (moment_gu, average_gu, weight_gu)
    )
    return (
        out_tokens,
        grad_tokens,
        grad_norm,
        moment_qkvu,
        moment_out,
        moment_gu,
        moment_down,
        average_qkvu,
        average_out,
        average_gu,
        average_down,
        weight_qkvu,
        weight_out,
        weight_gu,
        weight_down,
    )


def solution(mesh):
    rows = P(("dp", "head"), None)
    by_row = P(None, None, "dp", "head")
    by_column = P(None, "head", "dp")
    weights = (by_row, by_column, by_row, by_column)
    return jax.shard_map(
        per_device,
        mesh=mesh,
        in_specs=(rows, P("dp", None), P()) + weights * 3,
        out_specs=(rows, rows, P()) + weights * 3,
        check_vma=False,
    )
```
